128 devices in a mesh: sample: 2 (over x_lo), row: 8 (over y, core), col: 8 (over z, x_hi).
Axes of the slice: x: 4 (x_hi: 2, x_lo: 2; x = x_hi * 2 + x_lo), y: 4, z: 4, core: 2. Of those that a mesh axis runs over, the one named last changes fastest.
Arguments:
- images: bfloat16 [2, 512, 32768], P('sample', 'row', 'col'), may hold values from -6 to 6
- first_weight: bfloat16 [576, 128], replicated, may hold values from -0.25 to 0.25
- deep_weight: bfloat16 [1152, 256], P(None, 'col'), may hold values from -0.1875 to 0.1875
- deep_cotangent: bfloat16 [2, 256, 128, 128], P('sample', 'col', 'row'), may hold values from -0.046875 to 0.046875
Outputs:
- first_grad_weight: float32 [576, 128], replicated
- deep_grad_weight: float32 [1152, 256], P('row', 'col')
The draws below stay inside these ranges and needn't reach their ends.
All inputs are finite; a program needn't handle non-finite values.
Results may differ from the reference program's by a relative error of at most 0.0059.
Values may be sent and summed in bfloat16 or wider, within the bound.
A program may use at most 64 MiB of HBM per device.

```python
import jax
import jax.numpy as jnp

C0 = 64
C1 = 128
C2 = 256
TILE = 64
BATCH = 2
HEIGHT = 512
WIDTH = 512
N_SAMPLE = 2
N_ROW = 8


def shard_levels(own_key, extent, split, least, high):
    factor_of = 1.0
    for position, parts in split:
        draws = jax.random.uniform(jax.random.fold_in(jax.random.fold_in(own_key, 6), position), (parts,), jnp.float32, least / len(split), high / len(split))
        factor_of = factor_of * jnp.repeat(jnp.exp(draws), extent[position] // parts).reshape((-1,) + (1,) * (len(extent) - 1 - position))
    return factor_of


def centred(rng, shape, scale, limit, cuts=(), held_as=jnp.bfloat16):
    loudness = shard_levels(rng, shape, cuts, -0.22, 0.18) if cuts else 1.0
    drawn = jax.random.normal(rng, shape, jnp.float32) * scale * loudness
    return jnp.minimum(jnp.maximum(drawn, -limit), limit).astype(held_as)


def setup_inputs(seed: int = 0) -> dict:
    keys = jax.random.split(jax.random.key(seed), 5)
    images = centred(keys[0], (BATCH, HEIGHT, WIDTH * C0), 1.0, 6.0, ((0, 2), (1, 8), (2, 8)))
    first_weight = centred(keys[1], (C0 * 9, C1), (C0 * 9) ** -0.5, 0.25)
    deep_weight = centred(keys[2], (C1 * 9, C2), (C1 * 9) ** -0.5, 0.1875, ((1, 8),))
    deep_cotangent = centred(keys[3], (BATCH, C2, HEIGHT // 4, WIDTH // 4), (4.0 / (TILE * N_ROW)), 0.046875, ((0, 2), (1, 8), (2, 8)))
    return {"images": images, "first_weight": first_weight, "deep_weight": deep_weight, "deep_cotangent": deep_cotangent}


def taps_of(padded, out_rows, out_cols):
    pieces = []
    for row_off in range(3):
        for col_off in range(3):
            pieces.append(padded[:, row_off:row_off + 2 * out_rows:2, col_off:col_off + 2 * out_cols:2])
    return jnp.stack(pieces, 1)

def patch_matrix(field):
    channels = field.shape[0]
    padded = jnp.pad(field, ((0, 0), (1, 0), (1, 0)))
    return taps_of(padded, field.shape[1] // 2, field.shape[2] // 2).reshape(channels * 9, -1)

def silu_slope(value):
    logistic = jax.nn.sigmoid(value)
    return logistic * (1.0 + value * (1.0 - logistic))

def scatter_back(patch_grad, shape):
    unused, pull = jax.vjp(patch_matrix, jnp.zeros(shape, jnp.float32))
    return pull(patch_grad)[0]

def reference(images, first_weight, deep_weight, deep_cotangent):
    first_flat = first_weight.T
    deep_flat = deep_weight.T
    grad_first = jnp.zeros((C1, C0 * 9), jnp.float32)
    grad_deep = jnp.zeros((C2, C1 * 9), jnp.float32)
    for sample_index in range(N_SAMPLE):
        field = images[sample_index].reshape(HEIGHT, WIDTH, C0).transpose(2, 0, 1)
        first_patches = patch_matrix(field)
        first_pre = jnp.dot(first_flat, first_patches, preferred_element_type=jnp.float32)
        first_pre = first_pre.reshape(C1, HEIGHT // 2, WIDTH // 2)
        first_act = jax.nn.silu(first_pre).astype(jnp.bfloat16)
        deep_patches = patch_matrix(first_act)
        deep_pre = jnp.dot(deep_flat, deep_patches, preferred_element_type=jnp.float32)
        cotangent = deep_cotangent[sample_index].reshape(C2, -1).astype(jnp.float32)
        deep_grad = (cotangent * silu_slope(deep_pre)).astype(jnp.bfloat16)
        grad_deep = grad_deep + jnp.dot(deep_grad, deep_patches.T, preferred_element_type=jnp.float32)
        patch_grad = jnp.dot(deep_flat.T, deep_grad, preferred_element_type=jnp.float32)
        act_grad = scatter_back(patch_grad, first_act.shape).astype(jnp.bfloat16)
        first_grad = (act_grad.astype(jnp.float32) * silu_slope(first_pre)).astype(jnp.bfloat16)
        grad_first = grad_first + jnp.dot(first_grad.reshape(C1, -1), first_patches.T, preferred_element_type=jnp.float32)
    return (grad_first.T, grad_deep.T)
```

```python
import jax
import jax.numpy as jnp
from jax import lax
from jax.experimental import pallas as pl
from jax.experimental.pallas import tpu as pltpu
from jax.sharding import PartitionSpec as P

C0 = 64
C1 = 128
BF = jnp.bfloat16
F32 = jnp.float32
MESH = pl.DeviceIdType.MESH


def nn(a, b):
    return lax.dot_general(a, b, (((1,), (0,)), ((), ())), preferred_element_type=F32)


def nt(a, b):
    return lax.dot_general(a, b, (((1,), (1,)), ((), ())), preferred_element_type=F32)


def tn(a, b):
    return lax.dot_general(a, b, (((0,), (0,)), ((), ())), preferred_element_type=F32)


def eye(rows, cols):
    i = lax.broadcasted_iota(jnp.int32, (rows, cols), 0)
    j = lax.broadcasted_iota(jnp.int32, (rows, cols), 1)
    return (i == j).astype(F32).astype(BF)


def at16(index, size):
    return pl.ds(pl.multiple_of(index * size, size), size)


class Exchange:
    def __init__(self, n, me, device, source, target, send, recv):
        self.n, self.me, self.device = n, me, device
        self.source, self.target, self.send, self.recv = source, target, send, recv

    def copy(self, k, slot):
        peer = lax.rem(self.me + k, self.n)
        where = self.me if slot is None else peer
        return pltpu.make_async_remote_copy(
            src_ref=self.source(peer),
            dst_ref=self.target(where),
            send_sem=self.send.at[k],
            recv_sem=self.recv.at[where],
            device_id=self.device(peer),
            device_id_type=MESH,
        )

    def loop(self, act):
        def body(k, carry):
            act(k)
            return carry

        lax.fori_loop(1, self.n, body, 0)

    def start(self):
        self.loop(lambda k: self.copy(k, None).start())

    def wait_recv(self):
        self.loop(lambda k: self.copy(k, "peer").wait_recv())

    def wait_send(self):
        self.loop(lambda k: self.copy(k, None).wait_send())


def kernel(
    img, w1, wd, cot, out1, out2,
    xe, xr, w1f, wf, wdf, wt, cotf, cs, cr, q, acte, acto, sle, slo, patch,
    gwt, ra, gt, ra2, sb, rb, sb2, rb2, gtall, o2,
    local_sem, halo_send, halo_recv, w_send, w_recv, c_send, c_recv, a_send, a_recv,
    a2_send, a2_recv, b_send, b_recv, b2_send, b2_recv, g_send, g_recv,
):
    n_sample, n_row, n_col = (lax.axis_size(name) for name in ("sample", "row", "col"))
    n_group = n_sample * n_row
    s, r, c = (lax.axis_index(name) for name in ("sample", "row", "col"))
    group = s * n_row + r

    def col_device(p):
        return (s, r, p)

    def group_device(p):
        return (p // n_row, lax.rem(p, n_row), c)

    own = pltpu.make_async_copy(
        img.at[0], xe.at[pl.ds(16, 64), pl.ds(256, 4096)], local_sem
    )
    own.start()

    barrier = pltpu.get_barrier_semaphore()

    def greet_col(k, carry):
        pl.semaphore_signal(
            barrier, inc=1, device_id=col_device(lax.rem(c + k, n_col)), device_id_type=MESH
        )
        return carry

    def greet_group(k, carry):
        pl.semaphore_signal(
            barrier, inc=1, device_id=group_device(lax.rem(group + k, n_group)), device_id_type=MESH
        )
        return carry

    lax.fori_loop(1, n_col, greet_col, 0)
    lax.fori_loop(1, n_group, greet_group, 0)
    down, right = lax.rem(r + 1, n_row), lax.rem(c + 1, n_col)
    up, left = lax.rem(r + n_row - 1, n_row), lax.rem(c + n_col - 1, n_col)
    for corner in ((s, down, right), (s, up, left)):
        pl.semaphore_signal(barrier, inc=1, device_id=corner, device_id_type=MESH)

    wdf[...] = jnp.zeros(wdf.shape, F32)
    wdf[:, 0:32] = wd[...].astype(F32)
    unit32 = eye(32, 128)
    for tap in range(9):
        piece = wdf[pl.ds(tap, 128, stride=9), :].astype(BF)
        wt[at16(c, 32), 128 * tap : 128 * tap + 128] = nt(unit32, piece).astype(BF)

    cotf[...] = cot[0].reshape(512, 128).astype(F32)
    unit128 = eye(128, 128)
    for g in range(4):
        rows = [cotf[pl.ds(4 * g + k, 32, stride=16), :] for k in range(4)]
        cs[g] = nt(unit128, jnp.concatenate(rows, 0).astype(BF)).astype(BF)
    cr[c] = cs[:, at16(c, 16), :]

    pl.semaphore_wait(barrier, (n_col - 1) + (n_group - 1) + 2)

    def halo(index, source, target, device):
        return pltpu.make_async_remote_copy(
            src_ref=source,
            dst_ref=target,
            send_sem=halo_send.at[index],
            recv_sem=halo_recv.at[index],
            device_id=device,
            device_id_type=MESH,
        )

    to_down = halo(0, img.at[0, pl.ds(48, 16), :], xe.at[pl.ds(0, 16), pl.ds(256, 4096)], (s, down, c))
    to_right = halo(1, img.at[0, :, pl.ds(3840, 256)], xe.at[pl.ds(16, 64), pl.ds(0, 256)], (s, r, right))
    to_corner = halo(
        2, img.at[0, pl.ds(48, 16), pl.ds(3840, 256)], xe.at[pl.ds(0, 16), pl.ds(0, 256)], (s, down, right)
    )
    sends_down, sends_right = r < n_row - 1, c < n_col - 1
    has_up, has_left = r > 0, c > 0

    @pl.when(sends_down)
    def _():
        to_down.start()

    @pl.when(sends_right)
    def _():
        to_right.start()

    @pl.when(jnp.logical_and(sends_down, sends_right))
    def _():
        to_corner.start()

    weights = Exchange(
        n_col, c, col_device, lambda p: wt.at[at16(c, 32), :], lambda p: wt.at[at16(p, 32), :], w_send, w_recv
    )
    cotangents = Exchange(
        n_col, c, col_device, lambda p: cs.at[:, at16(p, 16), :], lambda p: cr.at[p], c_send, c_recv
    )
    weights.start()
    cotangents.start()

    @pl.when(jnp.logical_not(has_up))
    def _():
        xe[0:16, 256:4352] = jnp.zeros((16, 4096), BF)

    @pl.when(jnp.logical_not(has_left))
    def _():
        xe[16:80, 0:256] = jnp.zeros((64, 256), BF)

    @pl.when(jnp.logical_not(jnp.logical_and(has_up, has_left)))
    def _():
        xe[0:16, 0:256] = jnp.zeros((16, 256), BF)

    w1f[...] = w1[...].astype(F32)
    for ta in range(3):
        wf[ta, 0:64] = jnp.zeros((64, 128), BF)
        for tb in range(3):
            wf[ta, 64 * tb + 64 : 64 * tb + 128] = w1f[pl.ds(3 * ta + tb, 64, stride=9), :].astype(BF)

    own.wait()

    @pl.when(has_up)
    def _():
        to_down.wait_recv()

    @pl.when(has_left)
    def _():
        to_right.wait_recv()

    @pl.when(jnp.logical_and(has_up, has_left))
    def _():
        to_corner.wait_recv()

    row = lax.broadcasted_iota(jnp.int32, (112, 80), 0)
    col = lax.broadcasted_iota(jnp.int32, (112, 80), 1)
    pick = (col == 13 + 4 * (row % 16) + row // 16).astype(F32).astype(BF)
    for t in range(17):
        got = nn(pick, xe[:, 256 * t : 256 * t + 256]).astype(BF)
        xr[:, t] = got.reshape(7, 16, 256)

    def even_of(p):
        return xr[p].reshape(272, 256)

    def odd_of(p):
        return jnp.concatenate([xr[p, 0:16, :, 128:256], xr[p, 1:17, :, 0:128]], 2).reshape(256, 256)

    for a in range(3):
        even = nn(even_of(2 * a), wf[0]) + nn(even_of(2 * a + 1), wf[1]) + nn(even_of(2 * a + 2), wf[2])
        odd = nn(odd_of(2 * a), wf[0]) + nn(odd_of(2 * a + 1), wf[1]) + nn(odd_of(2 * a + 2), wf[2])
        for pre, act, slope, count in ((even, acte, sle, 17), (odd, acto, slo, 16)):
            sig = jax.nn.sigmoid(pre)
            act[a] = (pre * sig).astype(BF).reshape(count, 16, 128)
            slope[a] = (sig * (1.0 + pre * (1.0 - sig))).reshape(count, 16, 128)

    for a in range(3):
        patch[:, 384 * a : 384 * a + 128] = acte[a, 0:16].reshape(256, 128)
        patch[:, 384 * a + 128 : 384 * a + 256] = acto[a].reshape(256, 128)
        patch[:, 384 * a + 256 : 384 * a + 384] = acte[a, 1:17].reshape(256, 128)

    weights.wait_recv()
    pre = nt(patch[...], wt[...])

    cotangents.wait_recv()
    lane = lax.broadcasted_iota(jnp.int32, (16, 128), 1) // 32
    for g in range(4):
        for half in range(2):
            tiles = [cr[4 * half + i, g].astype(F32) for i in range(4)]
            for k in range(4):
                mixed = jnp.zeros((16, 128), F32)
                for i in range(4):
                    shift = (32 * (i - k)) % 128
                    moved = pltpu.roll(tiles[i], shift, 1) if shift else tiles[i]
                    mixed = jnp.where(lane == i, moved, mixed)
                q[half, 16 * (4 * g + k) : 16 * (4 * g + k) + 16] = mixed
    cotangent = jnp.concatenate(
        [
            jnp.concatenate([q[half, pl.ds(n, 16, stride=16), :] for half in range(2)], 1)
            for n in range(16)
        ],
        0,
    )

    sig = jax.nn.sigmoid(pre)
    dg = (cotangent * (sig * (1.0 + pre * (1.0 - sig)))).astype(BF)

    gwt[...] = tn(dg, patch[...]).astype(BF)
    deep_a = Exchange(
        n_col, c, col_device, lambda p: gwt.at[at16(p, 32), :], lambda p: ra.at[p], a_send, a_recv
    )
    deep_a.start()
    ra[c] = gwt[at16(c, 32), :]

    back = nn(dg, wt[...])
    empty = jnp.zeros((1, 16, 128), F32)
    totals = [jnp.zeros((128, 256), F32) for _ in range(3)]
    for a in range(3):
        part = [back[:, 384 * a + 128 * b : 384 * a + 128 * b + 128].reshape(16, 16, 128) for b in range(3)]
        even = jnp.concatenate([part[0], empty], 0) + jnp.concatenate([empty, part[2]], 0)
        even = (even * sle[a]).reshape(272, 128).astype(BF)
        odd = (part[1] * slo[a]).reshape(256, 128).astype(BF)
        for ta in range(3):
            totals[ta] += tn(even, even_of(2 * a + ta)) + tn(odd, odd_of(2 * a + ta))
    for ta in range(3):
        gt[:, 256 * ta : 256 * ta + 256] = totals[ta].astype(BF)
    first_a = Exchange(
        n_col, c, col_device, lambda p: gt.at[at16(p, 16), :], lambda p: ra2.at[p], a2_send, a2_recv
    )
    first_a.start()
    ra2[c] = gt[at16(c, 16), :]

    deep_a.wait_recv()
    total = ra[0].astype(F32)
    for p in range(1, n_col):
        total = total + ra[p].astype(F32)
    for g in range(3):
        taps = range(4 * g, min(4 * g + 4, 9))
        block = [total[:, 128 * tap : 128 * tap + 128] for tap in taps]
        if len(block) < 4:
            block.append(jnp.zeros((128 - 32 * len(block), 128), F32))
        sb[g] = nt(unit128, jnp.concatenate(block, 0).astype(BF)).astype(BF)
    deep_b = Exchange(
        n_group, group, group_device,
        lambda p: sb.at[:, at16(lax.rem(p, n_row), 16), :], lambda p: rb.at[p], b_send, b_recv,
    )
    deep_b.start()
    rb[group] = sb[:, at16(r, 16), :]

    first_a.wait_recv()
    total = ra2[0].astype(F32)
    for p in range(1, n_col):
        total = total + ra2[p].astype(F32)
    sb2[...] = total.astype(BF)
    first_b = Exchange(n_group, group, group_device, lambda p: sb2, lambda p: rb2.at[p], b2_send, b2_recv)
    first_b.start()
    rb2[group] = sb2[...]

    deep_b.wait_recv()
    total = rb[0].astype(F32)
    for p in range(1, n_group):
        total = total + rb[p].astype(F32)
    for tap in range(9):
        block = total[tap // 4]
        if tap % 4:
            block = pltpu.roll(block, 128 - 32 * (tap % 4), 1)
        o2[pl.ds(tap, 16, stride=9), :] = block
    out2[...] = o2[:, 0:32]

    first_b.wait_recv()
    total = rb2[0].astype(F32)
    for p in range(1, n_group):
        total = total + rb2[p].astype(F32)
    gtall[at16(c, 16), :] = total.astype(BF)
    first_g = Exchange(
        n_col, c, col_device,
        lambda p: gtall.at[at16(c, 16), :], lambda p: gtall.at[at16(p, 16), :], g_send, g_recv,
    )
    first_g.start()
    first_g.wait_recv()
    unit256 = eye(256, 256)
    for ta in range(3):
        block = nt(unit256, gtall[:, 256 * ta : 256 * ta + 256])
        for tb in range(3):
            out1[pl.ds(3 * ta + tb, 64, stride=9), :] = block[64 * tb + 64 : 64 * tb + 128]

    @pl.when(sends_down)
    def _():
        to_down.wait_send()

    @pl.when(sends_right)
    def _():
        to_right.wait_send()

    @pl.when(jnp.logical_and(sends_down, sends_right))
    def _():
        to_corner.wait_send()

    for exchange in (weights, cotangents, deep_a, first_a, deep_b, first_b, first_g):
        exchange.wait_send()


def on_device(images, first_weight, deep_weight, deep_cotangent):
    n_col = lax.axis_size("col")
    n_group = lax.axis_size("row") * lax.axis_size("sample")
    vmem = pl.BlockSpec(memory_space=pltpu.VMEM)
    dma = pltpu.SemaphoreType.DMA
    return pl.pallas_call(
        kernel,
        out_shape=(
            jax.ShapeDtypeStruct((576, 128), F32),
            jax.ShapeDtypeStruct((144, 32), F32),
        ),
        in_specs=[pl.BlockSpec(memory_space=pl.ANY), vmem, vmem, vmem],
        out_specs=(vmem, vmem),
        scratch_shapes=[
            pltpu.VMEM((80, 4352), BF),
            pltpu.VMEM((7, 17, 16, 256), BF),
            pltpu.VMEM((576, 128), F32),
            pltpu.VMEM((3, 256, 128), BF),
            pltpu.VMEM((1152, 128), F32),
            pltpu.VMEM((256, 1152), BF),
            pltpu.VMEM((512, 128), F32),
            pltpu.VMEM((4, 128, 128), BF),
            pltpu.VMEM((n_col, 4, 16, 128), BF),
            pltpu.VMEM((2, 256, 128), F32),
            pltpu.VMEM((3, 17, 16, 128), BF),
            pltpu.VMEM((3, 16, 16, 128), BF),
            pltpu.VMEM((3, 17, 16, 128), F32),
            pltpu.VMEM((3, 16, 16, 128), F32),
            pltpu.VMEM((256, 1152), BF),
            pltpu.VMEM((256, 1152), BF),
            pltpu.VMEM((n_col, 32, 1152), BF),
            pltpu.VMEM((128, 768), BF),
            pltpu.VMEM((n_col, 16, 768), BF),
            pltpu.VMEM((3, 128, 128), BF),
            pltpu.VMEM((n_group, 3, 16, 128), BF),
            pltpu.VMEM((16, 768), BF),
            pltpu.VMEM((n_group, 16, 768), BF),
            pltpu.VMEM((128, 768), BF),
            pltpu.VMEM((144, 128), F32),
            dma,
            dma((3,)), dma((3,)),
            dma((n_col,)), dma((n_col,)),
            dma((n_col,)), dma((n_col,)),
            dma((n_col,)), dma((n_col,)),
            dma((n_col,)), dma((n_col,)),
            dma((n_group,)), dma((n_group,)),
            dma((n_group,)), dma((n_group,)),
            dma((n_col,)), dma((n_col,)),
        ],
        compiler_params=pltpu.CompilerParams(
            collective_id=0, has_side_effects=True, vmem_limit_bytes=40 * 2**20
        ),
    )(images, first_weight, deep_weight, deep_cotangent)


def solution(mesh):
    return jax.shard_map(
        on_device,
        mesh=mesh,
        in_specs=(P("sample", "row", "col"), P(), P(None, "col"), P("sample", "col", "row", None)),
        out_specs=(P(), P("row", "col")),
        check_vma=False,
    )
```

```python
import jax
import jax.numpy as jnp
from jax import lax
from jax.experimental import pallas as pl
from jax.experimental.pallas import tpu as pltpu
from jax.sharding import PartitionSpec as P

BF = jnp.bfloat16
F32 = jnp.float32
MESH = pl.DeviceIdType.MESH

N_ROW = 8
N_COL = 8
N_BOTH = 16


def nn(a, b):
    return lax.dot_general(a, b, (((1,), (0,)), ((), ())), preferred_element_type=F32)


def nt(a, b):
    return lax.dot_general(a, b, (((1,), (1,)), ((), ())), preferred_element_type=F32)


def tn(a, b):
    return lax.dot_general(a, b, (((0,), (0,)), ((), ())), preferred_element_type=F32)


def eye(size):
    i = lax.broadcasted_iota(jnp.int32, (size, size), 0)
    j = lax.broadcasted_iota(jnp.int32, (size, size), 1)
    return (i == j).astype(F32).astype(BF)


def rows_of(index, size):
    return pl.ds(pl.multiple_of(index * size, size), size)


def remote(src, dst, send, recv, device):
    return pltpu.make_async_remote_copy(
        src_ref=src, dst_ref=dst, send_sem=send, recv_sem=recv, device_id=device, device_id_type=MESH
    )


class Fan:
    def __init__(self, pairs):
        self.pairs = list(pairs)

    def start(self):
        for out, _ in self.pairs:
            out.start()

    def wait_recv(self):
        for _, arriving in self.pairs:
            arriving.wait_recv()

    def wait_send(self):
        for out, _ in self.pairs:
            out.wait_send()


def kernel(
    img, w1, wd, cot, out1, out2,
    xe, w1v, wdv, cotv, xr, w1f, wf, wdf, wt, cotf, cs, cr, q, acte, acto, sle, slo, patch,
    gwt, pair_in, half, ra, gt, fa, sb, rb, sb2, rb2, gtall, o2,
    in_sem, halo_s, halo_r, w_s, w_r, v_s, v_r, c_s, c_r, d0_s, d0_r, d1_s, d1_r, d2_s, d2_r,
    f1_s, f1_r, f2_s, f2_r, f3_s, f3_r,
):
    s, r, c = (lax.axis_index(name) for name in ("sample", "row", "col"))
    core = lax.rem(r, 2)
    partner = r + 1 - 2 * core
    group = s * N_ROW + r
    plane = s * N_COL + c

    inputs = [
        pltpu.make_async_copy(cot.at[0], cotv, in_sem.at[0]),
        pltpu.make_async_copy(wd, wdv, in_sem.at[1]),
        pltpu.make_async_copy(w1, w1v, in_sem.at[2]),
        pltpu.make_async_copy(img.at[0], xe.at[pl.ds(16, 64), pl.ds(256, 4096)], in_sem.at[3]),
    ]

    def in_plane(k, sign=1):
        return (lax.rem(s + k // N_COL, 2), lax.rem(c + N_COL + sign * (k % N_COL), N_COL))

    def in_group(k, sign=1):
        return (lax.rem(s + k // N_ROW, 2), lax.rem(r + N_ROW + sign * (k % N_ROW), N_ROW))

    down, right = lax.rem(r + 1, N_ROW), lax.rem(c + 1, N_COL)
    up, left = lax.rem(r + N_ROW - 1, N_ROW), lax.rem(c + N_COL - 1, N_COL)

    barrier = pltpu.get_barrier_semaphore()
    greeted = [(s, down, right), (s, up, left)]
    for k in range(1, N_BOTH):
        ps, pc = in_plane(k)
        greeted.append((ps, r, pc))
    for k in range(1, N_BOTH):
        if k != N_ROW:
            ps, pr = in_group(k)
            greeted.append((ps, pr, c))
    for device in greeted:
        pl.semaphore_signal(barrier, inc=1, device_id=device, device_id_type=MESH)
    for copy in inputs:
        copy.start()

    unit = eye(128)

    inputs[0].wait()
    cotf[...] = cotv[...].reshape(512, 128).astype(F32)
    for g in range(4):
        picked = [cotf[pl.ds(4 * g + k, 32, stride=16), :] for k in range(4)]
        cs[g] = nt(unit, jnp.concatenate(picked, 0).astype(BF)).astype(BF)
    cr[0] = cs[:, rows_of(c, 16), :]

    inputs[1].wait()
    blank = jnp.zeros((96, 128), BF)
    for j in range(9):
        wdf[128 * j : 128 * j + 128] = nt(unit, jnp.concatenate([wdv[:, 128 * j : 128 * j + 128], blank], 0))
    for tap in range(9):
        piece = wdf[pl.ds(tap, 128, stride=9), :].astype(BF)
        wt[rows_of(c, 32), 128 * tap : 128 * tap + 128] = nt(unit, piece)[0:32].astype(BF)

    inputs[2].wait()
    w1f[...] = w1v[...].astype(F32)
    for ta in range(3):
        wf[ta, 0:64] = jnp.zeros((64, 128), BF)
        for tb in range(3):
            wf[ta, 64 * tb + 64 : 64 * tb + 128] = w1f[pl.ds(3 * ta + tb, 64, stride=9), :].astype(BF)

    pl.semaphore_wait(barrier, len(greeted))

    def halo(index, source, target, device):
        return remote(source, target, halo_s.at[index], halo_r.at[index], device)

    to_down = halo(0, img.at[0, pl.ds(48, 16), :], xe.at[pl.ds(0, 16), pl.ds(256, 4096)], (s, down, c))
    to_right = halo(1, img.at[0, :, pl.ds(3840, 256)], xe.at[pl.ds(16, 64), pl.ds(0, 256)], (s, r, right))
    to_corner = halo(
        2, img.at[0, pl.ds(48, 16), pl.ds(3840, 256)], xe.at[pl.ds(0, 16), pl.ds(0, 256)], (s, down, right)
    )
    sends_down, sends_right = r < N_ROW - 1, c < N_COL - 1
    has_up, has_left = r > 0, c > 0

    @pl.when(jnp.logical_and(sends_down, sends_right))
    def _():
        to_corner.start()

    @pl.when(sends_right)
    def _():
        to_right.start()

    z, xhi = c // 2, lax.rem(c, 2)

    def across(dz, dx, sign=1):
        return lax.rem(s + dx, 2), lax.rem(z + 4 + sign * dz, 4) * 2 + lax.rem(xhi + dx, 2)

    def half_shard(col, which):
        return wt.at[pl.ds(pl.multiple_of(32 * col + 16 * which, 16), 16), :]

    far_first = ((2, 1), (1, 1), (3, 1), (2, 0), (1, 0), (3, 0), (0, 1))
    weights, handed_on = [], []
    for k, (dz, dx) in enumerate(far_first):
        ps, pc = across(dz, dx)
        qs, qc = across(dz, dx, -1)
        weights.append(
            (
                remote(half_shard(c, core), half_shard(c, core), w_s.at[k], w_r.at[k], (ps, r, pc)),
                remote(half_shard(qc, core), half_shard(qc, core), w_s.at[k], w_r.at[k], (qs, r, qc)),
            )
        )
        handed_on.append(
            (
                remote(half_shard(qc, core), half_shard(qc, core), v_s.at[k], v_r.at[k], (s, partner, c)),
                remote(half_shard(qc, 1 - core), half_shard(qc, 1 - core), v_s.at[k], v_r.at[k], (s, partner, c)),
            )
        )
    weights, handed_on = Fan(weights), Fan(handed_on)
    weights.start()

    @pl.when(sends_down)
    def _():
        to_down.start()

    cotangents = []
    for k, (dz, dx) in enumerate(far_first):
        _, pc = across(dz, dx)
        _, qc = across(dz, dx, -1)
        cotangents.append(
            (
                remote(cs.at[:, rows_of(pc, 16), :], cr.at[dz + 4 * dx], c_s.at[k], c_r.at[k], (s, r, pc)),
                remote(cs.at[:, rows_of(qc, 16), :], cr.at[dz + 4 * dx], c_s.at[k], c_r.at[k], (s, r, qc)),
            )
        )
    cotangents = Fan(cotangents)
    cotangents.start()

    @pl.when(jnp.logical_not(has_up))
    def _():
        xe[0:16, 256:4352] = jnp.zeros((16, 4096), BF)

    @pl.when(jnp.logical_not(has_left))
    def _():
        xe[16:80, 0:256] = jnp.zeros((64, 256), BF)

    @pl.when(jnp.logical_not(jnp.logical_and(has_up, has_left)))
    def _():
        xe[0:16, 0:256] = jnp.zeros((16, 256), BF)

    inputs[3].wait()

    @pl.when(has_up)
    def _():
        to_down.wait_recv()

    @pl.when(has_left)
    def _():
        to_right.wait_recv()

    @pl.when(jnp.logical_and(has_up, has_left))
    def _():
        to_corner.wait_recv()

    row = lax.broadcasted_iota(jnp.int32, (112, 80), 0)
    col = lax.broadcasted_iota(jnp.int32, (112, 80), 1)
    pick = (col == 13 + 4 * (row % 16) + row // 16).astype(F32).astype(BF)
    for t in range(17):
        got = nn(pick, xe[:, 256 * t : 256 * t + 256]).astype(BF)
        xr[:, t] = got.reshape(7, 16, 256)

    def even_of(p):
        return xr[p].reshape(272, 256)

    def odd_of(p):
        return jnp.concatenate([xr[p, 0:16, :, 128:256], xr[p, 1:17, :, 0:128]], 2).reshape(256, 256)

    for a in range(3):
        even = nn(even_of(2 * a), wf[0]) + nn(even_of(2 * a + 1), wf[1]) + nn(even_of(2 * a + 2), wf[2])
        odd = nn(odd_of(2 * a), wf[0]) + nn(odd_of(2 * a + 1), wf[1]) + nn(odd_of(2 * a + 2), wf[2])
        for pre, act, slope, count in ((even, acte, sle, 17), (odd, acto, slo, 16)):
            sig = jax.nn.sigmoid(pre)
            act[a] = (pre * sig).astype(BF).reshape(count, 16, 128)
            slope[a] = (sig * (1.0 + pre * (1.0 - sig))).reshape(count, 16, 128)

    for a in range(3):
        patch[:, 384 * a : 384 * a + 128] = acte[a, 0:16].reshape(256, 128)
        patch[:, 384 * a + 128 : 384 * a + 256] = acto[a].reshape(256, 128)
        patch[:, 384 * a + 256 : 384 * a + 384] = acte[a, 1:17].reshape(256, 128)

    for k in range(6, -1, -1):
        weights.pairs[k][1].wait_recv()
        handed_on.pairs[k][0].start()

    cotangents.wait_recv()
    lane = lax.broadcasted_iota(jnp.int32, (16, 128), 1)
    quarter = lane // 32
    def from_col(col):
        return lax.rem(z + 4 - col // 2, 4) + 4 * lax.rem(xhi + col % 2, 2)

    for half_of in range(2):
        slots = [from_col(4 * half_of + i) for i in range(4)]
        for g in range(4):
            tiles = [cr[slots[i], g].astype(F32) for i in range(4)]
            for k in range(4):
                mixed = jnp.zeros((16, 128), F32)
                for i in range(4):
                    shift = (32 * (i - k)) % 128
                    moved = pltpu.roll(tiles[i], shift, 1) if shift else tiles[i]
                    mixed = jnp.where(quarter == i, moved, mixed)
                q[half_of, 16 * (4 * g + k) : 16 * (4 * g + k) + 16] = mixed
    cotangent = jnp.concatenate(
        [jnp.concatenate([q[h, pl.ds(n, 16, stride=16), :] for h in range(2)], 1) for n in range(16)], 0
    )

    handed_on.wait_recv()
    pre = nt(patch[...], wt[...])
    sig = jax.nn.sigmoid(pre)
    dg = (cotangent * (sig * (1.0 + pre * (1.0 - sig)))).astype(BF)

    back = nn(dg, wt[...])
    empty = jnp.zeros((1, 16, 128), F32)
    totals = [jnp.zeros((128, 256), F32) for _ in range(3)]
    for a in range(3):
        part = [back[:, 384 * a + 128 * b : 384 * a + 128 * b + 128].reshape(16, 16, 128) for b in range(3)]
        even = jnp.concatenate([part[0], empty], 0) + jnp.concatenate([empty, part[2]], 0)
        odd = part[1]
        if a == 1:
            even, odd = even.astype(BF).astype(F32), odd.astype(BF).astype(F32)
        even = (even * sle[a]).reshape(272, 128).astype(BF)
        odd = (odd * slo[a]).reshape(256, 128).astype(BF)
        for ta in range(3):
            totals[ta] += tn(even, even_of(2 * a + ta)) + tn(odd, odd_of(2 * a + ta))
    for ta in range(3):
        gt[:, 128 * ta : 128 * ta + 128] = totals[ta][:, 128:256].astype(BF)
    low = lax.broadcasted_iota(jnp.int32, (128, 128), 1) < 64
    both = jnp.where(low, pltpu.roll(totals[1][:, 0:128], 64, 1), totals[0][:, 0:128])
    gt[:, 384:512] = both.astype(BF)
    gt[:, 512:640] = totals[2][:, 0:128].astype(BF)

    first1 = []
    for k in range(1, N_ROW):
        pr, qr = lax.rem(r + k, N_ROW), lax.rem(r + N_ROW - k, N_ROW)
        first1.append(
            (
                remote(gt.at[rows_of(pr, 16), :], fa.at[k], f1_s.at[k], f1_r.at[k], (s, pr, c)),
                remote(gt.at[rows_of(qr, 16), :], fa.at[k], f1_s.at[k], f1_r.at[k], (s, qr, c)),
            )
        )
    first1 = Fan(first1)
    first1.start()

    gwt[...] = tn(dg, patch[...]).astype(BF).reshape(8, 2, 16, 1152)
    pair = remote(gwt.at[:, 1 - core], pair_in, d0_s.at[0], d0_r.at[0], (s, partner, c))
    pair.start()
    pair.wait_recv()
    half[...] = (gwt[:, core].astype(F32) + pair_in[...].astype(F32)).astype(BF)

    deep1 = []
    for k, (dz, dx) in enumerate(far_first):
        ps, pc = across(dz, dx)
        qs, qc = across(dz, dx, -1)
        deep1.append(
            (
                remote(half.at[pc], ra.at[k], d1_s.at[k], d1_r.at[k], (ps, r, pc)),
                remote(half.at[qc], ra.at[k], d1_s.at[k], d1_r.at[k], (qs, r, qc)),
            )
        )
    deep1 = Fan(deep1)
    deep1.start()

    first1.wait_recv()
    total = gt[rows_of(r, 16), :].astype(F32)
    for k in range(1, N_ROW):
        total = total + fa[k].astype(F32)
    sb2[...] = total.astype(BF)
    first2 = []
    for k in range(N_BOTH - 1, 0, -1):
        ps, pc = in_plane(k)
        qs, qc = in_plane(k, -1)
        first2.append(
            (
                remote(sb2, rb2.at[plane], f2_s.at[k], f2_r.at[k], (ps, r, pc)),
                remote(sb2, rb2.at[qs * N_COL + qc], f2_s.at[k], f2_r.at[k], (qs, r, qc)),
            )
        )
    first2 = Fan(first2)
    first2.start()
    rb2[plane] = sb2[...]

    deep1.wait_recv()
    total = half[c].astype(F32)
    for k in range(7):
        total = total + ra[k].astype(F32)
    block = jnp.concatenate([total[:, 128 * tap : 128 * tap + 128] for tap in range(8)], 0)
    sb[0] = nt(unit, block.astype(BF)).astype(BF)
    block = jnp.concatenate([total[:, 1024:1152], jnp.zeros((112, 128), F32)], 0)
    sb[1] = nt(unit, block.astype(BF)).astype(BF)
    deep2 = []
    for k in range(N_BOTH - 1, 0, -1):
        ps, pr = in_group(k)
        qs, qr = in_group(k, -1)
        deep2.append(
            (
                remote(sb.at[:, rows_of(pr, 16), :], rb.at[group], d2_s.at[k], d2_r.at[k], (ps, pr, c)),
                remote(
                    sb.at[:, rows_of(qr, 16), :], rb.at[qs * N_ROW + qr], d2_s.at[k], d2_r.at[k], (qs, qr, c)
                ),
            )
        )
    deep2 = Fan(deep2)
    deep2.start()
    rb[group] = sb[:, rows_of(r, 16), :]

    first2.wait_recv()
    total = rb2[0].astype(F32)
    for p in range(1, N_BOTH):
        total = total + rb2[p].astype(F32)
    gtall[rows_of(r, 16), :] = total.astype(BF)
    first3 = []
    for k in range(1, N_ROW):
        pr, qr = lax.rem(r + k, N_ROW), lax.rem(r + N_ROW - k, N_ROW)
        first3.append(
            (
                remote(gtall.at[rows_of(r, 16), :], gtall.at[rows_of(r, 16), :], f3_s.at[k], f3_r.at[k], (s, pr, c)),
                remote(gtall.at[rows_of(qr, 16), :], gtall.at[rows_of(qr, 16), :], f3_s.at[k], f3_r.at[k], (s, qr, c)),
            )
        )
    first3 = Fan(first3)
    first3.start()

    deep2.wait_recv()
    halves = []
    for which in range(2):
        total = rb[which].astype(F32)
        for p in range(which + 2, N_BOTH, 2):
            total = total + rb[p].astype(F32)
        halves.append(total)
    for tap in range(9):
        lower, upper = (h[tap // 8] for h in halves)
        shift = (128 - 16 * (tap % 8)) % 128
        lower = pltpu.roll(lower, shift, 1) if shift else lower
        upper = pltpu.roll(upper, (shift + 16) % 128, 1) if (shift + 16) % 128 else upper
        o2[pl.ds(tap, 16, stride=9), :] = jnp.where(lane < 16, lower, upper)
    out2[...] = o2[...].T[0:32, 0:144]

    first3.wait_recv()
    places = ((0, 1), (0, 2), (1, 1), (1, 2), (2, 1), (2, 2), (1, 0), (0, 0), None, (2, 0))
    for j in range(5):
        block = nt(unit, gtall[:, 128 * j : 128 * j + 128])
        for i in range(2):
            place = places[2 * j + i]
            if place is not None:
                out1[pl.ds(3 * place[0] + place[1], 64, stride=9), :] = block[64 * i : 64 * i + 64]

    @pl.when(sends_down)
    def _():
        to_down.wait_send()

    @pl.when(sends_right)
    def _():
        to_right.wait_send()

    @pl.when(jnp.logical_and(sends_down, sends_right))
    def _():
        to_corner.wait_send()

    pair.wait_send()
    for fan in (weights, handed_on, cotangents, first1, deep1, first2, deep2, first3):
        fan.wait_send()


def on_device(images, first_weight, deep_weight, deep_cotangent):
    anywhere = pl.BlockSpec(memory_space=pl.ANY)
    vmem = pl.BlockSpec(memory_space=pltpu.VMEM)

    def dma(count):
        return [pltpu.SemaphoreType.DMA((count,))] * 2

    first, deep = pl.pallas_call(
        kernel,
        out_shape=(jax.ShapeDtypeStruct((576, 128), F32), jax.ShapeDtypeStruct((32, 144), F32)),
        in_specs=[anywhere] * 4,
        out_specs=(vmem, vmem),
        scratch_shapes=[
            pltpu.VMEM((80, 4352), BF),
            pltpu.VMEM((576, 128), BF),
            pltpu.VMEM((32, 1152), BF),
            pltpu.VMEM((32, 16, 128), BF),
            pltpu.VMEM((7, 17, 16, 256), BF),
            pltpu.VMEM((576, 128), F32),
            pltpu.VMEM((3, 256, 128), BF),
            pltpu.VMEM((1152, 128), F32),
            pltpu.VMEM((256, 1152), BF),
            pltpu.VMEM((512, 128), F32),
            pltpu.VMEM((4, 128, 128), BF),
            pltpu.VMEM((8, 4, 16, 128), BF),
            pltpu.VMEM((2, 256, 128), F32),
            pltpu.VMEM((3, 17, 16, 128), BF),
            pltpu.VMEM((3, 16, 16, 128), BF),
            pltpu.VMEM((3, 17, 16, 128), F32),
            pltpu.VMEM((3, 16, 16, 128), F32),
            pltpu.VMEM((256, 1152), BF),
            pltpu.VMEM((8, 2, 16, 1152), BF),
            pltpu.VMEM((8, 16, 1152), BF),
            pltpu.VMEM((8, 16, 1152), BF),
            pltpu.VMEM((7, 16, 1152), BF),
            pltpu.VMEM((128, 640), BF),
            pltpu.VMEM((8, 16, 640), BF),
            pltpu.VMEM((2, 128, 128), BF),
            pltpu.VMEM((16, 2, 16, 128), BF),
            pltpu.VMEM((16, 640), BF),
            pltpu.VMEM((16, 16, 640), BF),
            pltpu.VMEM((128, 640), BF),
            pltpu.VMEM((256, 128), F32),
            pltpu.SemaphoreType.DMA((4,)),
            *dma(3), *dma(7), *dma(7), *dma(7), *dma(1), *dma(7), *dma(16), *dma(8), *dma(16), *dma(8),
        ],
        compiler_params=pltpu.CompilerParams(
            collective_id=0, has_side_effects=True, vmem_limit_bytes=60 * 2**20
        ),
    )(images, first_weight, deep_weight.T, deep_cotangent)
    return first, deep.T


def solution(mesh):
    return jax.shard_map(
        on_device,
        mesh=mesh,
        in_specs=(P("sample", "row", "col"), P(), P(None, "col"), P("sample", "col", "row", None)),
        out_specs=(P(), P("row", "col")),
        check_vma=False,
    )
```

```python
import jax
import jax.numpy as jnp
from jax import lax
from jax.experimental import pallas as pl
from jax.experimental.pallas import tpu as pltpu
from jax.sharding import PartitionSpec as P

BF = jnp.bfloat16
F32 = jnp.float32
MESH = pl.DeviceIdType.MESH

N_ROW = 8
N_COL = 8
N_BOTH = 16


def nn(a, b):
    return lax.dot_general(a, b, (((1,), (0,)), ((), ())), preferred_element_type=F32)


def nt(a, b):
    return lax.dot_general(a, b, (((1,), (1,)), ((), ())), preferred_element_type=F32)


def tn(a, b):
    return lax.dot_general(a, b, (((0,), (0,)), ((), ())), preferred_element_type=F32)


def eye(size):
    i = lax.broadcasted_iota(jnp.int32, (size, size), 0)
    j = lax.broadcasted_iota(jnp.int32, (size, size), 1)
    return (i == j).astype(F32).astype(BF)


def rows_of(index, size):
    return pl.ds(pl.multiple_of(index * size, size), size)


def remote(src, dst, send, recv, device):
    return pltpu.make_async_remote_copy(
        src_ref=src, dst_ref=dst, send_sem=send, recv_sem=recv, device_id=device, device_id_type=MESH
    )


class Fan:
    def __init__(self, pairs):
        self.pairs = list(pairs)

    def start(self):
        for out, _ in self.pairs:
            out.start()

    def wait_recv(self):
        for _, arriving in self.pairs:
            arriving.wait_recv()

    def wait_send(self):
        for out, _ in self.pairs:
            out.wait_send()


def kernel(
    img, w1, wd, cot, first_sum, deep_sum,
    xe, w1v, wdv, cotv, xr, w1f, wf, wdf, wt, cotf, cs, cr, q, acte, acto, sle, slo, patch,
    gw, pair_in, half, ra, gt, fa, sb, rb, sb2, rb2, gtall,
    in_sem, halo_s, halo_r, w_s, w_r, v_s, v_r, c_s, c_r, d0_s, d0_r, d1_s, d1_r, d2_s, d2_r,
    f1_s, f1_r, f2_s, f2_r, f3_s, f3_r,
):
    s, r, c = (lax.axis_index(name) for name in ("sample", "row", "col"))
    core = lax.rem(r, 2)
    partner = r + 1 - 2 * core
    plane = s * N_COL + c

    inputs = [
        pltpu.make_async_copy(cot.at[0], cotv, in_sem.at[0]),
        pltpu.make_async_copy(wd, wdv, in_sem.at[1]),
        pltpu.make_async_copy(w1, w1v, in_sem.at[2]),
        pltpu.make_async_copy(img.at[0], xe.at[pl.ds(16, 64), pl.ds(256, 4096)], in_sem.at[3]),
    ]

    def in_plane(k, sign=1):
        return (lax.rem(s + k // N_COL, 2), lax.rem(c + N_COL + sign * (k % N_COL), N_COL))

    down, right = lax.rem(r + 1, N_ROW), lax.rem(c + 1, N_COL)
    up, left = lax.rem(r + N_ROW - 1, N_ROW), lax.rem(c + N_COL - 1, N_COL)

    barrier = pltpu.get_barrier_semaphore()
    greeted = [(s, down, right), (s, up, left)]
    for k in range(1, N_BOTH):
        ps, pc = in_plane(k)
        greeted.append((ps, r, pc))
    for k in range(1, N_ROW):
        greeted.append((s, lax.rem(r + k, N_ROW), c))
    for device in greeted:
        pl.semaphore_signal(barrier, inc=1, device_id=device, device_id_type=MESH)
    for copy in inputs:
        copy.start()

    unit = eye(128)

    inputs[0].wait()
    cotf[...] = cotv[...].reshape(512, 128).astype(F32)
    for g in range(4):
        picked = [cotf[pl.ds(4 * g + k, 32, stride=16), :] for k in range(4)]
        cs[g] = nt(unit, jnp.concatenate(picked, 0).astype(BF)).astype(BF)
    cr[0] = cs[:, rows_of(c, 16), :]

    inputs[1].wait()
    blank = jnp.zeros((96, 128), BF)
    for j in range(9):
        wdf[128 * j : 128 * j + 128] = nt(unit, jnp.concatenate([wdv[:, 128 * j : 128 * j + 128], blank], 0))
    for tap in range(9):
        piece = wdf[pl.ds(tap, 128, stride=9), :].astype(BF)
        wt[rows_of(c, 32), 128 * tap : 128 * tap + 128] = nt(unit, piece)[0:32].astype(BF)

    inputs[2].wait()
    w1f[...] = w1v[...].astype(F32)
    for ta in range(3):
        wf[ta, 0:64] = jnp.zeros((64, 128), BF)
        for tb in range(3):
            wf[ta, 64 * tb + 64 : 64 * tb + 128] = w1f[pl.ds(3 * ta + tb, 64, stride=9), :].astype(BF)

    pl.semaphore_wait(barrier, len(greeted))

    def halo(index, source, target, device):
        return remote(source, target, halo_s.at[index], halo_r.at[index], device)

    to_down = halo(0, img.at[0, pl.ds(48, 16), :], xe.at[pl.ds(0, 16), pl.ds(256, 4096)], (s, down, c))
    to_right = halo(1, img.at[0, :, pl.ds(3840, 256)], xe.at[pl.ds(16, 64), pl.ds(0, 256)], (s, r, right))
    to_corner = halo(
        2, img.at[0, pl.ds(48, 16), pl.ds(3840, 256)], xe.at[pl.ds(0, 16), pl.ds(0, 256)], (s, down, right)
    )
    sends_down, sends_right = r < N_ROW - 1, c < N_COL - 1
    has_up, has_left = r > 0, c > 0

    @pl.when(jnp.logical_and(sends_down, sends_right))
    def _():
        to_corner.start()

    @pl.when(sends_right)
    def _():
        to_right.start()

    z, xhi = c // 2, lax.rem(c, 2)

    def across(dz, dx, sign=1):
        return lax.rem(s + dx, 2), lax.rem(z + 4 + sign * dz, 4) * 2 + lax.rem(xhi + dx, 2)

    def half_shard(col, which):
        return wt.at[pl.ds(pl.multiple_of(32 * col + 16 * which, 16), 16), :]

    far_first = ((2, 1), (1, 1), (3, 1), (2, 0), (1, 0), (3, 0), (0, 1))
    weights, handed_on = [], []
    for k, (dz, dx) in enumerate(far_first):
        ps, pc = across(dz, dx)
        qs, qc = across(dz, dx, -1)
        weights.append(
            (
                remote(half_shard(c, core), half_shard(c, core), w_s.at[k], w_r.at[k], (ps, r, pc)),
                remote(half_shard(qc, core), half_shard(qc, core), w_s.at[k], w_r.at[k], (qs, r, qc)),
            )
        )
        handed_on.append(
            (
                remote(half_shard(qc, core), half_shard(qc, core), v_s.at[k], v_r.at[k], (s, partner, c)),
                remote(half_shard(qc, 1 - core), half_shard(qc, 1 - core), v_s.at[k], v_r.at[k], (s, partner, c)),
            )
        )
    weights, handed_on = Fan(weights), Fan(handed_on)
    weights.start()

    @pl.when(sends_down)
    def _():
        to_down.start()

    cotangents = []
    for k, (dz, dx) in enumerate(far_first):
        _, pc = across(dz, dx)
        _, qc = across(dz, dx, -1)
        cotangents.append(
            (
                remote(cs.at[:, rows_of(pc, 16), :], cr.at[dz + 4 * dx], c_s.at[k], c_r.at[k], (s, r, pc)),
                remote(cs.at[:, rows_of(qc, 16), :], cr.at[dz + 4 * dx], c_s.at[k], c_r.at[k], (s, r, qc)),
            )
        )
    cotangents = Fan(cotangents)
    cotangents.start()

    @pl.when(jnp.logical_not(has_up))
    def _():
        xe[0:16, 256:4352] = jnp.zeros((16, 4096), BF)

    @pl.when(jnp.logical_not(has_left))
    def _():
        xe[16:80, 0:256] = jnp.zeros((64, 256), BF)

    @pl.when(jnp.logical_not(jnp.logical_and(has_up, has_left)))
    def _():
        xe[0:16, 0:256] = jnp.zeros((16, 256), BF)

    inputs[3].wait()

    @pl.when(has_up)
    def _():
        to_down.wait_recv()

    @pl.when(has_left)
    def _():
        to_right.wait_recv()

    @pl.when(jnp.logical_and(has_up, has_left))
    def _():
        to_corner.wait_recv()

    row = lax.broadcasted_iota(jnp.int32, (112, 80), 0)
    col = lax.broadcasted_iota(jnp.int32, (112, 80), 1)
    pick = (col == 13 + 4 * (row % 16) + row // 16).astype(F32).astype(BF)
    for t in range(17):
        got = nn(pick, xe[:, 256 * t : 256 * t + 256]).astype(BF)
        xr[:, t] = got.reshape(7, 16, 256)

    def even_of(p):
        return xr[p].reshape(272, 256)

    def odd_of(p):
        return jnp.concatenate([xr[p, 0:16, :, 128:256], xr[p, 1:17, :, 0:128]], 2).reshape(256, 256)

    for a in range(3):
        even = nn(even_of(2 * a), wf[0]) + nn(even_of(2 * a + 1), wf[1]) + nn(even_of(2 * a + 2), wf[2])
        odd = nn(odd_of(2 * a), wf[0]) + nn(odd_of(2 * a + 1), wf[1]) + nn(odd_of(2 * a + 2), wf[2])
        for pre, act, slope, count in ((even, acte, sle, 17), (odd, acto, slo, 16)):
            sig = jax.nn.sigmoid(pre)
            act[a] = (pre * sig).astype(BF).reshape(count, 16, 128)
            slope[a] = (sig * (1.0 + pre * (1.0 - sig))).reshape(count, 16, 128)

    for a in range(3):
        patch[:, 384 * a : 384 * a + 128] = acte[a, 0:16].reshape(256, 128)
        patch[:, 384 * a + 128 : 384 * a + 256] = acto[a].reshape(256, 128)
        patch[:, 384 * a + 256 : 384 * a + 384] = acte[a, 1:17].reshape(256, 128)

    for k in range(6, -1, -1):
        weights.pairs[k][1].wait_recv()
        handed_on.pairs[k][0].start()

    cotangents.wait_recv()
    quarter = lax.broadcasted_iota(jnp.int32, (16, 128), 1) // 32
    def from_col(col):
        return lax.rem(z + 4 - col // 2, 4) + 4 * lax.rem(xhi + col % 2, 2)

    for half_of in range(2):
        slots = [from_col(4 * half_of + i) for i in range(4)]
        for g in range(4):
            tiles = [cr[slots[i], g].astype(F32) for i in range(4)]
            for k in range(4):
                mixed = jnp.zeros((16, 128), F32)
                for i in range(4):
                    shift = (32 * (i - k)) % 128
                    moved = pltpu.roll(tiles[i], shift, 1) if shift else tiles[i]
                    mixed = jnp.where(quarter == i, moved, mixed)
                q[half_of, 16 * (4 * g + k) : 16 * (4 * g + k) + 16] = mixed
    cotangent = jnp.concatenate(
        [jnp.concatenate([q[h, pl.ds(n, 16, stride=16), :] for h in range(2)], 1) for n in range(16)], 0
    )

    handed_on.wait_recv()
    pre = nt(patch[...], wt[...])
    sig = jax.nn.sigmoid(pre)
    dg = (cotangent * (sig * (1.0 + pre * (1.0 - sig)))).astype(BF)

    back = nn(dg, wt[...])
    empty = jnp.zeros((1, 16, 128), F32)
    totals = [jnp.zeros((128, 256), F32) for _ in range(3)]
    for a in range(3):
        part = [back[:, 384 * a + 128 * b : 384 * a + 128 * b + 128].reshape(16, 16, 128) for b in range(3)]
        even = jnp.concatenate([part[0], empty], 0) + jnp.concatenate([empty, part[2]], 0)
        odd = part[1]
        if a == 1:
            even, odd = even.astype(BF).astype(F32), odd.astype(BF).astype(F32)
        even = (even * sle[a]).reshape(272, 128).astype(BF)
        odd = (odd * slo[a]).reshape(256, 128).astype(BF)
        for ta in range(3):
            totals[ta] += tn(even, even_of(2 * a + ta)) + tn(odd, odd_of(2 * a + ta))
    for ta in range(3):
        gt[:, 128 * ta : 128 * ta + 128] = totals[ta][:, 128:256].astype(BF)
    low = lax.broadcasted_iota(jnp.int32, (128, 128), 1) < 64
    both = jnp.where(low, pltpu.roll(totals[1][:, 0:128], 64, 1), totals[0][:, 0:128])
    gt[:, 384:512] = both.astype(BF)
    gt[:, 512:640] = totals[2][:, 0:128].astype(BF)

    first1 = []
    for k in range(1, N_ROW):
        pr, qr = lax.rem(r + k, N_ROW), lax.rem(r + N_ROW - k, N_ROW)
        first1.append(
            (
                remote(gt.at[rows_of(pr, 16), :], fa.at[k], f1_s.at[k], f1_r.at[k], (s, pr, c)),
                remote(gt.at[rows_of(qr, 16), :], fa.at[k], f1_s.at[k], f1_r.at[k], (s, qr, c)),
            )
        )
    first1 = Fan(first1)
    first1.start()

    gw[...] = tn(patch[...], dg).astype(BF).reshape(9, 4, 2, 16, 256)
    pair = remote(gw.at[:, :, 1 - core], pair_in, d0_s.at[0], d0_r.at[0], (s, partner, c))
    pair.start()
    pair.wait_recv()
    half[...] = (gw[:, :, core].astype(F32) + pair_in[...].astype(F32)).astype(BF)

    y = r // 2
    deep1 = []
    for k in (2, 1, 3):
        py, qy = lax.rem(y + k, 4), lax.rem(y + 4 - k, 4)
        deep1.append(
            (
                remote(half.at[:, py], ra.at[k], d1_s.at[k], d1_r.at[k], (s, 2 * py + core, c)),
                remote(half.at[:, qy], ra.at[k], d1_s.at[k], d1_r.at[k], (s, 2 * qy + core, c)),
            )
        )
    deep1 = Fan(deep1)
    deep1.start()

    first1.wait_recv()
    total = gt[rows_of(r, 16), :].astype(F32)
    for k in range(1, N_ROW):
        total = total + fa[k].astype(F32)
    sb2[...] = total.astype(BF)
    first2 = []
    for k in range(N_BOTH - 1, 0, -1):
        ps, pc = in_plane(k)
        qs, qc = in_plane(k, -1)
        first2.append(
            (
                remote(sb2, rb2.at[plane], f2_s.at[k], f2_r.at[k], (ps, r, pc)),
                remote(sb2, rb2.at[qs * N_COL + qc], f2_s.at[k], f2_r.at[k], (qs, r, qc)),
            )
        )
    first2 = Fan(first2)
    first2.start()
    rb2[plane] = sb2[...]

    deep1.wait_recv()
    total = half[:, y].astype(F32)
    for k in range(1, 4):
        total = total + ra[k].astype(F32)
    for h in range(2):
        block = total[0:8, :, 128 * h : 128 * h + 128].reshape(128, 128)
        sb[4 * h : 4 * h + 4, 0:2] = nt(unit, block.astype(BF)).astype(BF).reshape(4, 2, 16, 128)
        last = total[8, :, 128 * h : 128 * h + 128]
        for p in range(4):
            moved = pltpu.roll(last, 128 - 32 * p, 1) if p else last
            sb[4 * h + p, 2] = moved.astype(BF)
    deep2 = []
    for k in range(N_BOTH - 1, 0, -1):
        ps, pc = in_plane(k)
        qs, qc = in_plane(k, -1)
        deep2.append(
            (
                remote(sb.at[pc], rb.at[plane], d2_s.at[k], d2_r.at[k], (ps, r, pc)),
                remote(sb.at[qc], rb.at[qs * N_COL + qc], d2_s.at[k], d2_r.at[k], (qs, r, qc)),
            )
        )
    deep2 = Fan(deep2)
    deep2.start()
    rb[plane] = sb[c]

    first2.wait_recv()
    total = rb2[0].astype(F32)
    for p in range(1, N_BOTH):
        total = total + rb2[p].astype(F32)
    gtall[rows_of(r, 16), :] = total.astype(BF)
    first3 = []
    for k in range(1, N_ROW):
        pr, qr = lax.rem(r + k, N_ROW), lax.rem(r + N_ROW - k, N_ROW)
        first3.append(
            (
                remote(gtall.at[rows_of(r, 16), :], gtall.at[rows_of(r, 16), :], f3_s.at[k], f3_r.at[k], (s, pr, c)),
                remote(gtall.at[rows_of(qr, 16), :], gtall.at[rows_of(qr, 16), :], f3_s.at[k], f3_r.at[k], (s, qr, c)),
            )
        )
    first3 = Fan(first3)
    first3.start()

    deep2.wait_recv()
    total = rb[0].astype(F32)
    for p in range(1, N_BOTH):
        total = total + rb[p].astype(F32)
    deep_sum[...] = total

    first3.wait_recv()
    first_sum[...] = gtall[...]

    @pl.when(sends_down)
    def _():
        to_down.wait_send()

    @pl.when(sends_right)
    def _():
        to_right.wait_send()

    @pl.when(jnp.logical_and(sends_down, sends_right))
    def _():
        to_corner.wait_send()

    pair.wait_send()
    for fan in (weights, handed_on, cotangents, first1, deep1, first2, deep2, first3):
        fan.wait_send()


def finish(first_sum, deep_sum, out1, out2, o2):
    unit = eye(128)
    places = ((0, 1), (0, 2), (1, 1), (1, 2), (2, 1), (2, 2), (1, 0), (0, 0), None, (2, 0))
    for j in range(5):
        block = nt(unit, first_sum[:, 128 * j : 128 * j + 128])
        for i in range(2):
            place = places[2 * j + i]
            if place is not None:
                out1[pl.ds(3 * place[0] + place[1], 64, stride=9), :] = block[64 * i : 64 * i + 64]
    most = jnp.concatenate([deep_sum[0], deep_sum[1], jnp.zeros((96, 128), F32)], 0).T
    for tap in range(9):
        o2[pl.ds(tap, 16, stride=9), :] = most[16 * tap : 16 * tap + 16] if tap < 8 else deep_sum[2]
    out2[...] = o2[...].T[0:32, 0:144]


def on_device(images, first_weight, deep_weight, deep_cotangent):
    anywhere = pl.BlockSpec(memory_space=pltpu.HBM)
    vmem = pl.BlockSpec(memory_space=pltpu.VMEM)

    def dma(count):
        return [pltpu.SemaphoreType.DMA((count,))] * 2

    first, deep = pl.pallas_call(
        kernel,
        out_shape=(jax.ShapeDtypeStruct((128, 640), BF), jax.ShapeDtypeStruct((3, 16, 128), F32)),
        in_specs=[anywhere] * 4,
        out_specs=(vmem, vmem),
        scratch_shapes=[
            pltpu.VMEM((80, 4352), BF),
            pltpu.VMEM((576, 128), BF),
            pltpu.VMEM((32, 1152), BF),
            pltpu.VMEM((32, 16, 128), BF),
            pltpu.VMEM((7, 17, 16, 256), BF),
            pltpu.VMEM((576, 128), F32),
            pltpu.VMEM((3, 256, 128), BF),
            pltpu.VMEM((1152, 128), F32),
            pltpu.VMEM((256, 1152), BF),
            pltpu.VMEM((512, 128), F32),
            pltpu.VMEM((4, 128, 128), BF),
            pltpu.VMEM((8, 4, 16, 128), BF),
            pltpu.VMEM((2, 256, 128), F32),
            pltpu.VMEM((3, 17, 16, 128), BF),
            pltpu.VMEM((3, 16, 16, 128), BF),
            pltpu.VMEM((3, 17, 16, 128), F32),
            pltpu.VMEM((3, 16, 16, 128), F32),
            pltpu.VMEM((256, 1152), BF),
            pltpu.VMEM((9, 4, 2, 16, 256), BF),
            pltpu.VMEM((9, 4, 16, 256), BF),
            pltpu.VMEM((9, 4, 16, 256), BF),
            pltpu.VMEM((4, 9, 16, 256), BF),
            pltpu.VMEM((128, 640), BF),
            pltpu.VMEM((8, 16, 640), BF),
            pltpu.VMEM((8, 3, 16, 128), BF),
            pltpu.VMEM((16, 3, 16, 128), BF),
            pltpu.VMEM((16, 640), BF),
            pltpu.VMEM((16, 16, 640), BF),
            pltpu.VMEM((128, 640), BF),
            pltpu.SemaphoreType.DMA((4,)),
            *dma(3), *dma(7), *dma(7), *dma(7), *dma(1), *dma(4), *dma(16), *dma(8), *dma(16), *dma(8),
        ],
        compiler_params=pltpu.CompilerParams(
            collective_id=0, has_side_effects=True, vmem_limit_bytes=60 * 2**20
        ),
    )(images, first_weight, deep_weight.T, deep_cotangent)
    first, deep = pl.pallas_call(
        finish,
        out_shape=(jax.ShapeDtypeStruct((576, 128), F32), jax.ShapeDtypeStruct((32, 144), F32)),
        in_specs=[vmem, vmem],
        out_specs=(vmem, vmem),
        scratch_shapes=[pltpu.VMEM((256, 128), F32)],
        compiler_params=pltpu.CompilerParams(vmem_limit_bytes=60 * 2**20),
    )(first, deep)
    return first, deep.T


def solution(mesh):
    return jax.shard_map(
        on_device,
        mesh=mesh,
        in_specs=(P("sample", "row", "col"), P(), P(None, "col"), P("sample", "col", "row", None)),
        out_specs=(P(), P("row", "col")),
        check_vma=False,
    )
```

```python
import jax
import jax.numpy as jnp
from jax import lax
from jax.experimental import pallas as pl
from jax.experimental.pallas import tpu as pltpu
from jax.sharding import PartitionSpec as P

BF = jnp.bfloat16
F32 = jnp.float32
MESH = pl.DeviceIdType.MESH

HOPS = {(0, 0): 0, (0, 1): 1, (1, 1): 1, (1, 0): 2}
PLANE = sorted(
    ((dz, fx, fs) for dz in range(4) for fx in range(2) for fs in range(2) if dz + fx + fs),
    key=lambda step: -(min(step[0], 4 - step[0]) + HOPS[step[1:]]),
)
LINE = (4, 5, 3, 2, 6, 7, 1)
N_ROW = 8
N_COL = 8
N_BOTH = 16


def nn(a, b):
    return lax.dot_general(a, b, (((1,), (0,)), ((), ())), preferred_element_type=F32)


def nt(a, b):
    return lax.dot_general(a, b, (((1,), (1,)), ((), ())), preferred_element_type=F32)


def tn(a, b):
    return lax.dot_general(a, b, (((0,), (0,)), ((), ())), preferred_element_type=F32)


def eye(size):
    i = lax.broadcasted_iota(jnp.int32, (size, size), 0)
    j = lax.broadcasted_iota(jnp.int32, (size, size), 1)
    return (i == j).astype(F32).astype(BF)


def rows_of(index, size):
    return pl.ds(pl.multiple_of(index * size, size), size)


def remote(src, dst, send, recv, device):
    return pltpu.make_async_remote_copy(
        src_ref=src, dst_ref=dst, send_sem=send, recv_sem=recv, device_id=device, device_id_type=MESH
    )


class Fan:
    def __init__(self, pairs):
        self.pairs = list(pairs)

    def start(self):
        for out, _ in self.pairs:
            out.start()

    def wait_recv(self):
        for _, arriving in self.pairs:
            arriving.wait_recv()

    def wait_send(self):
        for out, _ in self.pairs:
            out.wait_send()


def kernel(
    img, w1, wd, cot, first_sum, deep_sum,
    xe, w1v, wdv, cotv, xr, w1f, wf, wdf, wt, cotf, cs, cr, q, acte, acto, sle, slo, patch,
    gw, pair_in, half, ra, gt, fa, sb, rb, sb2, rb2, gtall,
    in_sem, halo_s, halo_r, w_s, w_r, v_s, v_r, c_s, c_r, d0_s, d0_r, d1_s, d1_r, d2_s, d2_r,
    f1_s, f1_r, f2_s, f2_r, f3_s, f3_r,
):
    s, r, c = (lax.axis_index(name) for name in ("sample", "row", "col"))
    core = lax.rem(r, 2)
    partner = r + 1 - 2 * core
    plane = s * N_COL + c

    inputs = [
        pltpu.make_async_copy(cot.at[0], cotv, in_sem.at[0]),
        pltpu.make_async_copy(wd, wdv, in_sem.at[1]),
        pltpu.make_async_copy(w1, w1v, in_sem.at[2]),
        pltpu.make_async_copy(img.at[0], xe.at[pl.ds(16, 64), pl.ds(256, 4096)], in_sem.at[3]),
    ]

    z, xhi = c // 2, lax.rem(c, 2)

    def in_plane(step, sign=1):
        dz, fx, fs = step
        return lax.rem(s + fs, 2), lax.rem(z + 4 + sign * dz, 4) * 2 + lax.rem(xhi + fx, 2)

    down, right = lax.rem(r + 1, N_ROW), lax.rem(c + 1, N_COL)
    up, left = lax.rem(r + N_ROW - 1, N_ROW), lax.rem(c + N_COL - 1, N_COL)

    barrier = pltpu.get_barrier_semaphore()
    greeted = [(s, down, right), (s, up, left)]
    for step in PLANE:
        ps, pc = in_plane(step)
        greeted.append((ps, r, pc))
    for k in LINE:
        greeted.append((s, lax.rem(r + k, N_ROW), c))
    for device in greeted:
        pl.semaphore_signal(barrier, inc=1, device_id=device, device_id_type=MESH)
    for copy in inputs:
        copy.start()

    unit = eye(128)

    inputs[0].wait()
    cotf[...] = cotv[...].reshape(512, 128).astype(F32)
    for g in range(4):
        picked = [cotf[pl.ds(4 * g + k, 32, stride=16), :] for k in range(4)]
        cs[g] = nt(unit, jnp.concatenate(picked, 0).astype(BF)).astype(BF)
    cr[0] = cs[:, rows_of(c, 16), :]

    inputs[1].wait()
    blank = jnp.zeros((96, 128), BF)
    for j in range(9):
        wdf[128 * j : 128 * j + 128] = nt(unit, jnp.concatenate([wdv[:, 128 * j : 128 * j + 128], blank], 0))
    for tap in range(9):
        piece = wdf[pl.ds(tap, 128, stride=9), :].astype(BF)
        wt[rows_of(c, 32), 128 * tap : 128 * tap + 128] = nt(unit, piece)[0:32].astype(BF)

    inputs[2].wait()
    w1f[...] = w1v[...].astype(F32)
    for ta in range(3):
        wf[ta, 0:64] = jnp.zeros((64, 128), BF)
        for tb in range(3):
            wf[ta, 64 * tb + 64 : 64 * tb + 128] = w1f[pl.ds(3 * ta + tb, 64, stride=9), :].astype(BF)

    pl.semaphore_wait(barrier, len(greeted))

    def halo(index, source, target, device):
        return remote(source, target, halo_s.at[index], halo_r.at[index], device)

    to_down = halo(0, img.at[0, pl.ds(48, 16), :], xe.at[pl.ds(0, 16), pl.ds(256, 4096)], (s, down, c))
    to_right = halo(1, img.at[0, :, pl.ds(3840, 256)], xe.at[pl.ds(16, 64), pl.ds(0, 256)], (s, r, right))
    to_corner = halo(
        2, img.at[0, pl.ds(48, 16), pl.ds(3840, 256)], xe.at[pl.ds(0, 16), pl.ds(0, 256)], (s, down, right)
    )
    sends_down, sends_right = r < N_ROW - 1, c < N_COL - 1
    has_up, has_left = r > 0, c > 0

    @pl.when(jnp.logical_and(sends_down, sends_right))
    def _():
        to_corner.start()

    @pl.when(sends_right)
    def _():
        to_right.start()

    def across(dz, dx, sign=1):
        return in_plane((dz, dx, dx), sign)

    def half_shard(col, which):
        return wt.at[pl.ds(pl.multiple_of(32 * col + 16 * which, 16), 16), :]

    far_first = ((2, 1), (1, 1), (3, 1), (2, 0), (1, 0), (3, 0), (0, 1))
    weights, handed_on = [], []
    for k, (dz, dx) in enumerate(far_first):
        ps, pc = across(dz, dx)
        qs, qc = across(dz, dx, -1)
        weights.append(
            (
                remote(half_shard(c, core), half_shard(c, core), w_s.at[k], w_r.at[k], (ps, r, pc)),
                remote(half_shard(qc, core), half_shard(qc, core), w_s.at[k], w_r.at[k], (qs, r, qc)),
            )
        )
        handed_on.append(
            (
                remote(half_shard(qc, core), half_shard(qc, core), v_s.at[k], v_r.at[k], (s, partner, c)),
                remote(half_shard(qc, 1 - core), half_shard(qc, 1 - core), v_s.at[k], v_r.at[k], (s, partner, c)),
            )
        )
    weights, handed_on = Fan(weights), Fan(handed_on)
    weights.start()

    @pl.when(sends_down)
    def _():
        to_down.start()

    cotangents = []
    for k, (dz, dx) in enumerate(far_first):
        _, pc = across(dz, dx)
        _, qc = across(dz, dx, -1)
        cotangents.append(
            (
                remote(cs.at[:, rows_of(pc, 16), :], cr.at[dz + 4 * dx], c_s.at[k], c_r.at[k], (s, r, pc)),
                remote(cs.at[:, rows_of(qc, 16), :], cr.at[dz + 4 * dx], c_s.at[k], c_r.at[k], (s, r, qc)),
            )
        )
    cotangents = Fan(cotangents)
    cotangents.start()

    @pl.when(jnp.logical_not(has_up))
    def _():
        xe[0:16, 256:4352] = jnp.zeros((16, 4096), BF)

    @pl.when(jnp.logical_not(has_left))
    def _():
        xe[16:80, 0:256] = jnp.zeros((64, 256), BF)

    @pl.when(jnp.logical_not(jnp.logical_and(has_up, has_left)))
    def _():
        xe[0:16, 0:256] = jnp.zeros((16, 256), BF)

    for k in range(6, -1, -1):
        weights.pairs[k][1].wait_recv()
        handed_on.pairs[k][0].start()

    inputs[3].wait()

    @pl.when(has_up)
    def _():
        to_down.wait_recv()

    @pl.when(has_left)
    def _():
        to_right.wait_recv()

    @pl.when(jnp.logical_and(has_up, has_left))
    def _():
        to_corner.wait_recv()

    row = lax.broadcasted_iota(jnp.int32, (112, 80), 0)
    col = lax.broadcasted_iota(jnp.int32, (112, 80), 1)
    pick = (col == 13 + 4 * (row % 16) + row // 16).astype(F32).astype(BF)
    for t in range(17):
        got = nn(pick, xe[:, 256 * t : 256 * t + 256]).astype(BF)
        xr[:, t] = got.reshape(7, 16, 256)

    def even_of(p):
        return xr[p].reshape(272, 256)

    def odd_of(p):
        return jnp.concatenate([xr[p, 0:16, :, 128:256], xr[p, 1:17, :, 0:128]], 2).reshape(256, 256)

    for a in range(3):
        even = nn(even_of(2 * a), wf[0]) + nn(even_of(2 * a + 1), wf[1]) + nn(even_of(2 * a + 2), wf[2])
        odd = nn(odd_of(2 * a), wf[0]) + nn(odd_of(2 * a + 1), wf[1]) + nn(odd_of(2 * a + 2), wf[2])
        for pre, act, slope, count in ((even, acte, sle, 17), (odd, acto, slo, 16)):
            sig = jax.nn.sigmoid(pre)
            act[a] = (pre * sig).astype(BF).reshape(count, 16, 128)
            slope[a] = (sig * (1.0 + pre * (1.0 - sig))).reshape(count, 16, 128)

    for a in range(3):
        patch[:, 384 * a : 384 * a + 128] = acte[a, 0:16].reshape(256, 128)
        patch[:, 384 * a + 128 : 384 * a + 256] = acto[a].reshape(256, 128)
        patch[:, 384 * a + 256 : 384 * a + 384] = acte[a, 1:17].reshape(256, 128)

    cotangents.wait_recv()
    quarter = lax.broadcasted_iota(jnp.int32, (16, 128), 1) // 32
    def from_col(col):
        return lax.rem(z + 4 - col // 2, 4) + 4 * lax.rem(xhi + col % 2, 2)

    for half_of in range(2):
        slots = [from_col(4 * half_of + i) for i in range(4)]
        for g in range(4):
            tiles = [cr[slots[i], g].astype(F32) for i in range(4)]
            for k in range(4):
                mixed = jnp.zeros((16, 128), F32)
                for i in range(4):
                    shift = (32 * (i - k)) % 128
                    moved = pltpu.roll(tiles[i], shift, 1) if shift else tiles[i]
                    mixed = jnp.where(quarter == i, moved, mixed)
                q[half_of, 16 * (4 * g + k) : 16 * (4 * g + k) + 16] = mixed
    cotangent = jnp.concatenate(
        [jnp.concatenate([q[h, pl.ds(n, 16, stride=16), :] for h in range(2)], 1) for n in range(16)], 0
    )

    handed_on.wait_recv()
    pre = nt(patch[...], wt[...])
    sig = jax.nn.sigmoid(pre)
    dg = (cotangent * (sig * (1.0 + pre * (1.0 - sig)))).astype(BF)

    back = nn(dg, wt[...])
    empty = jnp.zeros((1, 16, 128), F32)
    totals = [jnp.zeros((128, 256), F32) for _ in range(3)]
    for a in range(3):
        part = [back[:, 384 * a + 128 * b : 384 * a + 128 * b + 128].reshape(16, 16, 128) for b in range(3)]
        even = jnp.concatenate([part[0], empty], 0) + jnp.concatenate([empty, part[2]], 0)
        odd = part[1]
        if a == 1:
            even, odd = even.astype(BF).astype(F32), odd.astype(BF).astype(F32)
        even = (even * sle[a]).reshape(272, 128).astype(BF)
        odd = (odd * slo[a]).reshape(256, 128).astype(BF)
        for ta in range(3):
            totals[ta] += tn(even, even_of(2 * a + ta)) + tn(odd, odd_of(2 * a + ta))
    for ta in range(3):
        gt[:, 128 * ta : 128 * ta + 128] = totals[ta][:, 128:256].astype(BF)
    low = lax.broadcasted_iota(jnp.int32, (128, 128), 1) < 64
    both = jnp.where(low, pltpu.roll(totals[1][:, 0:128], 64, 1), totals[0][:, 0:128])
    gt[:, 384:512] = both.astype(BF)
    gt[:, 512:640] = totals[2][:, 0:128].astype(BF)

    first1 = []
    for k in LINE:
        pr, qr = lax.rem(r + k, N_ROW), lax.rem(r + N_ROW - k, N_ROW)
        first1.append(
            (
                remote(gt.at[rows_of(pr, 16), :], fa.at[k], f1_s.at[k], f1_r.at[k], (s, pr, c)),
                remote(gt.at[rows_of(qr, 16), :], fa.at[k], f1_s.at[k], f1_r.at[k], (s, qr, c)),
            )
        )
    first1 = Fan(first1)
    first1.start()

    gw[...] = tn(patch[...], dg).astype(BF).reshape(9, 4, 2, 16, 256)
    pair = remote(gw.at[:, :, 1 - core], pair_in, d0_s.at[0], d0_r.at[0], (s, partner, c))
    pair.start()
    pair.wait_recv()
    half[...] = (gw[:, :, core].astype(F32) + pair_in[...].astype(F32)).astype(BF)

    y = r // 2
    deep1 = []
    for k in (2, 1, 3):
        py, qy = lax.rem(y + k, 4), lax.rem(y + 4 - k, 4)
        deep1.append(
            (
                remote(half.at[:, py], ra.at[k], d1_s.at[k], d1_r.at[k], (s, 2 * py + core, c)),
                remote(half.at[:, qy], ra.at[k], d1_s.at[k], d1_r.at[k], (s, 2 * qy + core, c)),
            )
        )
    deep1 = Fan(deep1)
    deep1.start()

    first1.wait_recv()
    total = gt[rows_of(r, 16), :].astype(F32)
    for k in range(1, N_ROW):
        total = total + fa[k].astype(F32)
    sb2[...] = total.astype(BF)
    first2 = []
    for k, step in enumerate(PLANE):
        ps, pc = in_plane(step)
        qs, qc = in_plane(step, -1)
        first2.append(
            (
                remote(sb2, rb2.at[plane], f2_s.at[k], f2_r.at[k], (ps, r, pc)),
                remote(sb2, rb2.at[qs * N_COL + qc], f2_s.at[k], f2_r.at[k], (qs, r, qc)),
            )
        )
    first2 = Fan(first2)
    first2.start()
    rb2[plane] = sb2[...]

    deep1.wait_recv()
    total = half[:, y].astype(F32)
    for k in range(1, 4):
        total = total + ra[k].astype(F32)
    for h in range(2):
        block = total[0:8, :, 128 * h : 128 * h + 128].reshape(128, 128)
        sb[4 * h : 4 * h + 4, 0:2] = nt(unit, block.astype(BF)).astype(BF).reshape(4, 2, 16, 128)
        last = total[8, :, 128 * h : 128 * h + 128]
        for p in range(4):
            moved = pltpu.roll(last, 128 - 32 * p, 1) if p else last
            sb[4 * h + p, 2] = moved.astype(BF)
    deep2 = []
    for k, step in enumerate(PLANE):
        ps, pc = in_plane(step)
        qs, qc = in_plane(step, -1)
        deep2.append(
            (
                remote(sb.at[pc], rb.at[plane], d2_s.at[k], d2_r.at[k], (ps, r, pc)),
                remote(sb.at[qc], rb.at[qs * N_COL + qc], d2_s.at[k], d2_r.at[k], (qs, r, qc)),
            )
        )
    deep2 = Fan(deep2)
    deep2.start()
    rb[plane] = sb[c]

    first2.wait_recv()
    total = rb2[0].astype(F32)
    for p in range(1, N_BOTH):
        total = total + rb2[p].astype(F32)
    gtall[rows_of(r, 16), :] = total.astype(BF)
    first3 = []
    for k in LINE:
        pr, qr = lax.rem(r + k, N_ROW), lax.rem(r + N_ROW - k, N_ROW)
        first3.append(
            (
                remote(gtall.at[rows_of(r, 16), :], gtall.at[rows_of(r, 16), :], f3_s.at[k], f3_r.at[k], (s, pr, c)),
                remote(gtall.at[rows_of(qr, 16), :], gtall.at[rows_of(qr, 16), :], f3_s.at[k], f3_r.at[k], (s, qr, c)),
            )
        )
    first3 = Fan(first3)
    first3.start()

    deep2.wait_recv()
    total = rb[0].astype(F32)
    for p in range(1, N_BOTH):
        total = total + rb[p].astype(F32)
    deep_sum[...] = total

    first3.wait_recv()
    first_sum[...] = gtall[...]

    @pl.when(sends_down)
    def _():
        to_down.wait_send()

    @pl.when(sends_right)
    def _():
        to_right.wait_send()

    @pl.when(jnp.logical_and(sends_down, sends_right))
    def _():
        to_corner.wait_send()

    pair.wait_send()
    for fan in (weights, handed_on, cotangents, first1, deep1, first2, deep2, first3):
        fan.wait_send()


def finish(first_sum, deep_sum, out1, out2, o2):
    unit = eye(128)
    places = ((0, 1), (0, 2), (1, 1), (1, 2), (2, 1), (2, 2), (1, 0), (0, 0), None, (2, 0))
    for j in range(5):
        block = nt(unit, first_sum[:, 128 * j : 128 * j + 128])
        for i in range(2):
            place = places[2 * j + i]
            if place is not None:
                out1[pl.ds(3 * place[0] + place[1], 64, stride=9), :] = block[64 * i : 64 * i + 64]
    most = jnp.concatenate([deep_sum[0], deep_sum[1], jnp.zeros((96, 128), F32)], 0).T
    for tap in range(9):
        o2[pl.ds(tap, 16, stride=9), :] = most[16 * tap : 16 * tap + 16] if tap < 8 else deep_sum[2]
    out2[...] = o2[...].T[0:32, 0:144]


def on_device(images, first_weight, deep_weight, deep_cotangent):
    anywhere = pl.BlockSpec(memory_space=pltpu.HBM)
    vmem = pl.BlockSpec(memory_space=pltpu.VMEM)

    def dma(count):
        return [pltpu.SemaphoreType.DMA((count,))] * 2

    first, deep = pl.pallas_call(
        kernel,
        out_shape=(jax.ShapeDtypeStruct((128, 640), BF), jax.ShapeDtypeStruct((3, 16, 128), F32)),
        in_specs=[anywhere] * 4,
        out_specs=(vmem, vmem),
        scratch_shapes=[
            pltpu.VMEM((80, 4352), BF),
            pltpu.VMEM((576, 128), BF),
            pltpu.VMEM((32, 1152), BF),
            pltpu.VMEM((32, 16, 128), BF),
            pltpu.VMEM((7, 17, 16, 256), BF),
            pltpu.VMEM((576, 128), F32),
            pltpu.VMEM((3, 256, 128), BF),
            pltpu.VMEM((1152, 128), F32),
            pltpu.VMEM((256, 1152), BF),
            pltpu.VMEM((512, 128), F32),
            pltpu.VMEM((4, 128, 128), BF),
            pltpu.VMEM((8, 4, 16, 128), BF),
            pltpu.VMEM((2, 256, 128), F32),
            pltpu.VMEM((3, 17, 16, 128), BF),
            pltpu.VMEM((3, 16, 16, 128), BF),
            pltpu.VMEM((3, 17, 16, 128), F32),
            pltpu.VMEM((3, 16, 16, 128), F32),
            pltpu.VMEM((256, 1152), BF),
            pltpu.VMEM((9, 4, 2, 16, 256), BF),
            pltpu.VMEM((9, 4, 16, 256), BF),
            pltpu.VMEM((9, 4, 16, 256), BF),
            pltpu.VMEM((4, 9, 16, 256), BF),
            pltpu.VMEM((128, 640), BF),
            pltpu.VMEM((8, 16, 640), BF),
            pltpu.VMEM((8, 3, 16, 128), BF),
            pltpu.VMEM((16, 3, 16, 128), BF),
            pltpu.VMEM((16, 640), BF),
            pltpu.VMEM((16, 16, 640), BF),
            pltpu.VMEM((128, 640), BF),
            pltpu.SemaphoreType.DMA((4,)),
            *dma(3), *dma(7), *dma(7), *dma(7), *dma(1), *dma(4), *dma(16), *dma(8), *dma(16), *dma(8),
        ],
        compiler_params=pltpu.CompilerParams(
            collective_id=0, has_side_effects=True, vmem_limit_bytes=60 * 2**20
        ),
    )(images, first_weight, deep_weight.T, deep_cotangent)
    first, deep = pl.pallas_call(
        finish,
        out_shape=(jax.ShapeDtypeStruct((576, 128), F32), jax.ShapeDtypeStruct((32, 144), F32)),
        in_specs=[vmem, vmem],
        out_specs=(vmem, vmem),
        scratch_shapes=[pltpu.VMEM((256, 128), F32)],
        compiler_params=pltpu.CompilerParams(vmem_limit_bytes=60 * 2**20),
    )(first, deep)
    return first, deep.T


def solution(mesh):
    return jax.shard_map(
        on_device,
        mesh=mesh,
        in_specs=(P("sample", "row", "col"), P(), P(None, "col"), P("sample", "col", "row", None)),
        out_specs=(P(), P("row", "col")),
        check_vma=False,
    )
```

```python
import jax
import jax.numpy as jnp
from jax import lax
from jax.experimental import pallas as pl
from jax.experimental.pallas import tpu as pltpu
from jax.sharding import PartitionSpec as P

BF = jnp.bfloat16
F32 = jnp.float32
MESH = pl.DeviceIdType.MESH

HOPS = {(0, 0): 0, (0, 1): 1, (1, 1): 1, (1, 0): 2}
PLANE = sorted(
    ((dz, fx, fs) for dz in range(4) for fx in range(2) for fs in range(2) if dz + fx + fs),
    key=lambda step: -(min(step[0], 4 - step[0]) + HOPS[step[1:]]),
)
LINE = (4, 5, 3, 2, 6, 7, 1)
N_ROW = 8
N_COL = 8
N_BOTH = 16


def nn(a, b):
    return lax.dot_general(a, b, (((1,), (0,)), ((), ())), preferred_element_type=F32)


def nt(a, b):
    return lax.dot_general(a, b, (((1,), (1,)), ((), ())), preferred_element_type=F32)


def tn(a, b):
    return lax.dot_general(a, b, (((0,), (0,)), ((), ())), preferred_element_type=F32)


def eye(size):
    i = lax.broadcasted_iota(jnp.int32, (size, size), 0)
    j = lax.broadcasted_iota(jnp.int32, (size, size), 1)
    return (i == j).astype(F32).astype(BF)


def rows_of(index, size):
    return pl.ds(pl.multiple_of(index * size, size), size)


def remote(src, dst, send, recv, device):
    return pltpu.make_async_remote_copy(
        src_ref=src, dst_ref=dst, send_sem=send, recv_sem=recv, device_id=device, device_id_type=MESH
    )


class Fan:
    def __init__(self, pairs):
        self.pairs = list(pairs)

    def start(self):
        for out, _ in self.pairs:
            out.start()

    def wait_recv(self):
        for _, arriving in self.pairs:
            arriving.wait_recv()

    def wait_send(self):
        for out, _ in self.pairs:
            out.wait_send()


def kernel(
    img, w1, wd, cot, first_sum, deep_sum,
    xe, w1v, wdv, cotv, xr, w1f, wf, wdf, wt, cotf, cs, cr, q, acte, acto, sle, slo, patch,
    gw, pair_in, half, ra, gt, fa, sb, rb, sb2, rb2, gtall,
    in_sem, halo_s, halo_r, w_s, w_r, v_s, v_r, c_s, c_r, d0_s, d0_r, d1_s, d1_r, d2_s, d2_r,
    f1_s, f1_r, f2_s, f2_r, f3_s, f3_r,
):
    s, r, c = (lax.axis_index(name) for name in ("sample", "row", "col"))
    core = lax.rem(r, 2)
    partner = r + 1 - 2 * core
    plane = s * N_COL + c

    inputs = [
        pltpu.make_async_copy(cot.at[0], cotv, in_sem.at[0]),
        pltpu.make_async_copy(wd, wdv, in_sem.at[1]),
        pltpu.make_async_copy(w1, w1v, in_sem.at[2]),
        pltpu.make_async_copy(img.at[0], xe.at[pl.ds(16, 64), pl.ds(256, 4096)], in_sem.at[3]),
    ]

    z, xhi = c // 2, lax.rem(c, 2)

    def in_plane(step, sign=1):
        dz, fx, fs = step
        return lax.rem(s + fs, 2), lax.rem(z + 4 + sign * dz, 4) * 2 + lax.rem(xhi + fx, 2)

    down, right = lax.rem(r + 1, N_ROW), lax.rem(c + 1, N_COL)
    up, left = lax.rem(r + N_ROW - 1, N_ROW), lax.rem(c + N_COL - 1, N_COL)

    barrier = pltpu.get_barrier_semaphore()
    greeted = [(s, down, right), (s, up, left)]
    for step in PLANE:
        ps, pc = in_plane(step)
        greeted.append((ps, r, pc))
    for k in LINE:
        greeted.append((s, lax.rem(r + k, N_ROW), c))
    for device in greeted:
        pl.semaphore_signal(barrier, inc=1, device_id=device, device_id_type=MESH)
    for copy in inputs:
        copy.start()

    unit = eye(128)

    inputs[0].wait()
    cotf[...] = cotv[...].reshape(512, 128).astype(F32)
    for g in range(4):
        picked = [cotf[pl.ds(4 * g + k, 32, stride=16), :] for k in range(4)]
        cs[g] = nt(unit, jnp.concatenate(picked, 0).astype(BF)).astype(BF)
    cr[0] = cs[:, rows_of(c, 16), :]

    inputs[1].wait()
    blank = jnp.zeros((96, 128), BF)
    for j in range(9):
        wdf[128 * j : 128 * j + 128] = nt(unit, jnp.concatenate([wdv[:, 128 * j : 128 * j + 128], blank], 0))
    for tap in range(9):
        piece = wdf[pl.ds(tap, 128, stride=9), :].astype(BF)
        wt[rows_of(c, 32), 128 * tap : 128 * tap + 128] = nt(unit, piece)[0:32].astype(BF)

    inputs[2].wait()
    w1f[...] = w1v[...].astype(F32)
    for ta in range(3):
        wf[ta, 0:64] = jnp.zeros((64, 128), BF)
        for tb in range(3):
            wf[ta, 64 * tb + 64 : 64 * tb + 128] = w1f[pl.ds(3 * ta + tb, 64, stride=9), :].astype(BF)

    pl.semaphore_wait(barrier, len(greeted))

    def halo(index, source, target, device):
        return remote(source, target, halo_s.at[index], halo_r.at[index], device)

    to_down = halo(0, img.at[0, pl.ds(48, 16), :], xe.at[pl.ds(0, 16), pl.ds(256, 4096)], (s, down, c))
    to_right = halo(1, img.at[0, :, pl.ds(3840, 256)], xe.at[pl.ds(16, 64), pl.ds(0, 256)], (s, r, right))
    to_corner = halo(
        2, img.at[0, pl.ds(48, 16), pl.ds(3840, 256)], xe.at[pl.ds(0, 16), pl.ds(0, 256)], (s, down, right)
    )
    sends_down, sends_right = r < N_ROW - 1, c < N_COL - 1
    has_up, has_left = r > 0, c > 0

    @pl.when(jnp.logical_and(sends_down, sends_right))
    def _():
        to_corner.start()

    @pl.when(sends_right)
    def _():
        to_right.start()

    def across(dz, dx, sign=1):
        return in_plane((dz, dx, dx), sign)

    def half_shard(col, which):
        return wt.at[pl.ds(pl.multiple_of(32 * col + 16 * which, 16), 16), :]

    far_first = ((2, 1), (1, 1), (3, 1), (2, 0), (1, 0), (3, 0), (0, 1))
    weights, handed_on = [], []
    for k, (dz, dx) in enumerate(far_first):
        ps, pc = across(dz, dx)
        qs, qc = across(dz, dx, -1)
        weights.append(
            (
                remote(half_shard(c, core), half_shard(c, core), w_s.at[k], w_r.at[k], (ps, r, pc)),
                remote(half_shard(qc, core), half_shard(qc, core), w_s.at[k], w_r.at[k], (qs, r, qc)),
            )
        )
        handed_on.append(
            (
                remote(half_shard(qc, core), half_shard(qc, core), v_s.at[k], v_r.at[k], (s, partner, c)),
                remote(half_shard(qc, 1 - core), half_shard(qc, 1 - core), v_s.at[k], v_r.at[k], (s, partner, c)),
            )
        )
    weights, handed_on = Fan(weights), Fan(handed_on)
    weights.start()

    @pl.when(sends_down)
    def _():
        to_down.start()

    cotangents = []
    for k, (dz, dx) in enumerate(far_first):
        _, pc = across(dz, dx)
        _, qc = across(dz, dx, -1)
        cotangents.append(
            (
                remote(cs.at[:, rows_of(pc, 16), :], cr.at[dz + 4 * dx], c_s.at[k], c_r.at[k], (s, r, pc)),
                remote(cs.at[:, rows_of(qc, 16), :], cr.at[dz + 4 * dx], c_s.at[k], c_r.at[k], (s, r, qc)),
            )
        )
    cotangents = Fan(cotangents)
    cotangents.start()

    @pl.when(jnp.logical_not(has_up))
    def _():
        xe[0:16, 256:4352] = jnp.zeros((16, 4096), BF)

    @pl.when(jnp.logical_not(has_left))
    def _():
        xe[16:80, 0:256] = jnp.zeros((64, 256), BF)

    @pl.when(jnp.logical_not(jnp.logical_and(has_up, has_left)))
    def _():
        xe[0:16, 0:256] = jnp.zeros((16, 256), BF)

    for k in range(6, -1, -1):
        weights.pairs[k][1].wait_recv()
        handed_on.pairs[k][0].start()

    inputs[3].wait()

    @pl.when(has_up)
    def _():
        to_down.wait_recv()

    @pl.when(has_left)
    def _():
        to_right.wait_recv()

    @pl.when(jnp.logical_and(has_up, has_left))
    def _():
        to_corner.wait_recv()

    row = lax.broadcasted_iota(jnp.int32, (112, 80), 0)
    col = lax.broadcasted_iota(jnp.int32, (112, 80), 1)
    pick = (col == 13 + 4 * (row % 16) + row // 16).astype(F32).astype(BF)
    for t in range(17):
        got = nn(pick, xe[:, 256 * t : 256 * t + 256]).astype(BF)
        xr[:, t] = got.reshape(7, 16, 256)

    def even_of(p):
        return xr[p].reshape(272, 256)

    def odd_of(p):
        return jnp.concatenate([xr[p, 0:16, :, 128:256], xr[p, 1:17, :, 0:128]], 2).reshape(256, 256)

    for a in range(3):
        even = nn(even_of(2 * a), wf[0]) + nn(even_of(2 * a + 1), wf[1]) + nn(even_of(2 * a + 2), wf[2])
        odd = nn(odd_of(2 * a), wf[0]) + nn(odd_of(2 * a + 1), wf[1]) + nn(odd_of(2 * a + 2), wf[2])
        for pre, act, slope, count in ((even, acte, sle, 17), (odd, acto, slo, 16)):
            sig = jax.nn.sigmoid(pre)
            act[a] = (pre * sig).astype(BF).reshape(count, 16, 128)
            slope[a] = (sig * (1.0 + pre * (1.0 - sig))).reshape(count, 16, 128)

    for a in range(3):
        patch[:, 384 * a : 384 * a + 128] = acte[a, 0:16].reshape(256, 128)
        patch[:, 384 * a + 128 : 384 * a + 256] = acto[a].reshape(256, 128)
        patch[:, 384 * a + 256 : 384 * a + 384] = acte[a, 1:17].reshape(256, 128)

    cotangents.wait_recv()
    quarter = lax.broadcasted_iota(jnp.int32, (16, 128), 1) // 32
    def from_col(col):
        return lax.rem(z + 4 - col // 2, 4) + 4 * lax.rem(xhi + col % 2, 2)

    for half_of in range(2):
        slots = [from_col(4 * half_of + i) for i in range(4)]
        for g in range(4):
            tiles = [cr[slots[i], g].astype(F32) for i in range(4)]
            for k in range(4):
                mixed = jnp.zeros((16, 128), F32)
                for i in range(4):
                    shift = (32 * (i - k)) % 128
                    moved = pltpu.roll(tiles[i], shift, 1) if shift else tiles[i]
                    mixed = jnp.where(quarter == i, moved, mixed)
                q[half_of, 16 * (4 * g + k) : 16 * (4 * g + k) + 16] = mixed
    cotangent = jnp.concatenate(
        [jnp.concatenate([q[h, pl.ds(n, 16, stride=16), :] for h in range(2)], 1) for n in range(16)], 0
    )

    handed_on.wait_recv()
    pre = nt(patch[...], wt[...])
    sig = jax.nn.sigmoid(pre)
    dg = (cotangent * (sig * (1.0 + pre * (1.0 - sig)))).astype(BF)

    back = nn(dg, wt[...])
    empty = jnp.zeros((1, 16, 128), F32)
    totals = [jnp.zeros((128, 256), F32) for _ in range(3)]
    for a in range(3):
        part = [back[:, 384 * a + 128 * b : 384 * a + 128 * b + 128].reshape(16, 16, 128) for b in range(3)]
        even = jnp.concatenate([part[0], empty], 0) + jnp.concatenate([empty, part[2]], 0)
        odd = part[1]
        if a == 1:
            even, odd = even.astype(BF).astype(F32), odd.astype(BF).astype(F32)
        even = (even * sle[a]).reshape(272, 128).astype(BF)
        odd = (odd * slo[a]).reshape(256, 128).astype(BF)
        for ta in range(3):
            totals[ta] += tn(even, even_of(2 * a + ta)) + tn(odd, odd_of(2 * a + ta))
    for ta in range(3):
        gt[:, 128 * ta : 128 * ta + 128] = totals[ta][:, 128:256].astype(BF)
    low = lax.broadcasted_iota(jnp.int32, (128, 128), 1) < 64
    both = jnp.where(low, pltpu.roll(totals[1][:, 0:128], 64, 1), totals[0][:, 0:128])
    gt[:, 384:512] = both.astype(BF)
    gt[:, 512:640] = totals[2][:, 0:128].astype(BF)

    first1 = []
    for k in LINE:
        pr, qr = lax.rem(r + k, N_ROW), lax.rem(r + N_ROW - k, N_ROW)
        first1.append(
            (
                remote(gt.at[rows_of(pr, 16), :], fa.at[k], f1_s.at[k], f1_r.at[k], (s, pr, c)),
                remote(gt.at[rows_of(qr, 16), :], fa.at[k], f1_s.at[k], f1_r.at[k], (s, qr, c)),
            )
        )
    first1 = Fan(first1)
    first1.start()

    gw[...] = tn(patch[...], dg).astype(BF).reshape(9, 4, 2, 16, 256)
    pair = remote(gw.at[:, :, 1 - core], pair_in, d0_s.at[0], d0_r.at[0], (s, partner, c))
    pair.start()
    pair.wait_recv()
    half[...] = (gw[:, :, core].astype(F32) + pair_in[...].astype(F32)).astype(BF)

    y = r // 2
    deep1 = []
    for k in (2, 1, 3):
        py, qy = lax.rem(y + k, 4), lax.rem(y + 4 - k, 4)
        deep1.append(
            (
                remote(half.at[:, py], ra.at[k], d1_s.at[k], d1_r.at[k], (s, 2 * py + core, c)),
                remote(half.at[:, qy], ra.at[k], d1_s.at[k], d1_r.at[k], (s, 2 * qy + core, c)),
            )
        )
    deep1 = Fan(deep1)
    deep1.start()

    first1.wait_recv()
    total = gt[rows_of(r, 16), :].astype(F32)
    for k in range(1, N_ROW):
        total = total + fa[k].astype(F32)
    sb2[...] = total.astype(BF)
    first2 = []
    for k, step in enumerate(PLANE):
        ps, pc = in_plane(step)
        qs, qc = in_plane(step, -1)
        first2.append(
            (
                remote(sb2, rb2.at[plane], f2_s.at[k], f2_r.at[k], (ps, r, pc)),
                remote(sb2, rb2.at[qs * N_COL + qc], f2_s.at[k], f2_r.at[k], (qs, r, qc)),
            )
        )
    first2 = Fan(first2)
    first2.start()
    rb2[plane] = sb2[...]

    deep1.wait_recv()
    total = half[:, y].astype(F32)
    for k in range(1, 4):
        total = total + ra[k].astype(F32)
    for h in range(2):
        block = total[0:8, :, 128 * h : 128 * h + 128].reshape(128, 128)
        sb[4 * h : 4 * h + 4, 0:2] = nt(unit, block.astype(BF)).astype(BF).reshape(4, 2, 16, 128)
        last = total[8, :, 128 * h : 128 * h + 128]
        for p in range(4):
            moved = pltpu.roll(last, 128 - 32 * p, 1) if p else last
            sb[4 * h + p, 2] = moved.astype(BF)
    deep2 = []
    for k, step in enumerate(PLANE):
        ps, pc = in_plane(step)
        qs, qc = in_plane(step, -1)
        deep2.append(
            (
                remote(sb.at[pc], rb.at[plane], d2_s.at[k], d2_r.at[k], (ps, r, pc)),
                remote(sb.at[qc], rb.at[qs * N_COL + qc], d2_s.at[k], d2_r.at[k], (qs, r, qc)),
            )
        )
    deep2 = Fan(deep2)
    deep2.start()
    rb[plane] = sb[c]

    first2.wait_recv()
    total = rb2[0].astype(F32)
    for p in range(1, N_BOTH):
        total = total + rb2[p].astype(F32)
    gtall[rows_of(r, 16), :] = total.astype(BF)
    first3 = []
    for k in LINE:
        pr, qr = lax.rem(r + k, N_ROW), lax.rem(r + N_ROW - k, N_ROW)
        first3.append(
            (
                remote(gtall.at[rows_of(r, 16), :], gtall.at[rows_of(r, 16), :], f3_s.at[k], f3_r.at[k], (s, pr, c)),
                remote(gtall.at[rows_of(qr, 16), :], gtall.at[rows_of(qr, 16), :], f3_s.at[k], f3_r.at[k], (s, qr, c)),
            )
        )
    first3 = Fan(first3)
    first3.start()

    deep2.wait_recv()
    total = rb[0].astype(F32)
    for p in range(1, N_BOTH):
        total = total + rb[p].astype(F32)
    deep_sum[...] = total

    first3.wait_recv()
    first_sum[...] = gtall[...]

    @pl.when(sends_down)
    def _():
        to_down.wait_send()

    @pl.when(sends_right)
    def _():
        to_right.wait_send()

    @pl.when(jnp.logical_and(sends_down, sends_right))
    def _():
        to_corner.wait_send()

    pair.wait_send()
    for fan in (weights, handed_on, cotangents, first1, deep1, first2, deep2, first3):
        fan.wait_send()


def finish(first_sum, deep_sum, out1, out2, o2):
    unit = eye(128)
    places = ((0, 1), (0, 2), (1, 1), (1, 2), (2, 1), (2, 2), (1, 0), (0, 0), None, (2, 0))
    for j in range(5):
        block = nt(unit, first_sum[:, 128 * j : 128 * j + 128])
        for i in range(2):
            place = places[2 * j + i]
            if place is not None:
                out1[pl.ds(3 * place[0] + place[1], 64, stride=9), :] = block[64 * i : 64 * i + 64]
    most = jnp.concatenate([deep_sum[0], deep_sum[1], jnp.zeros((96, 128), F32)], 0).T
    for tap in range(9):
        o2[pl.ds(tap, 16, stride=9), :] = most[16 * tap : 16 * tap + 16] if tap < 8 else deep_sum[2]
    out2[...] = o2[...].T[0:32, 0:144]


def on_device(images, first_weight, deep_weight, deep_cotangent):
    anywhere = pl.BlockSpec(memory_space=pltpu.HBM)
    vmem = pl.BlockSpec(memory_space=pltpu.VMEM)

    def dma(count):
        return [pltpu.SemaphoreType.DMA((count,))] * 2

    first, deep = pl.pallas_call(
        kernel,
        out_shape=(jax.ShapeDtypeStruct((128, 640), BF), jax.ShapeDtypeStruct((3, 16, 128), F32)),
        in_specs=[anywhere] * 4,
        out_specs=(vmem, vmem),
        scratch_shapes=[
            pltpu.VMEM((80, 4352), BF),
            pltpu.VMEM((576, 128), BF),
            pltpu.VMEM((32, 1152), BF),
            pltpu.VMEM((32, 16, 128), BF),
            pltpu.VMEM((7, 17, 16, 256), BF),
            pltpu.VMEM((576, 128), F32),
            pltpu.VMEM((3, 256, 128), BF),
            pltpu.VMEM((1152, 128), F32),
            pltpu.VMEM((256, 1152), BF),
            pltpu.VMEM((512, 128), F32),
            pltpu.VMEM((4, 128, 128), BF),
            pltpu.VMEM((8, 4, 16, 128), BF),
            pltpu.VMEM((2, 256, 128), F32),
            pltpu.VMEM((3, 17, 16, 128), BF),
            pltpu.VMEM((3, 16, 16, 128), BF),
            pltpu.VMEM((3, 17, 16, 128), F32),
            pltpu.VMEM((3, 16, 16, 128), F32),
            pltpu.VMEM((256, 1152), BF),
            pltpu.VMEM((9, 4, 2, 16, 256), BF),
            pltpu.VMEM((9, 4, 16, 256), BF),
            pltpu.VMEM((9, 4, 16, 256), BF),
            pltpu.VMEM((4, 9, 16, 256), BF),
            pltpu.VMEM((128, 640), BF),
            pltpu.VMEM((8, 16, 640), BF),
            pltpu.VMEM((8, 3, 16, 128), BF),
            pltpu.VMEM((16, 3, 16, 128), BF),
            pltpu.VMEM((16, 640), BF),
            pltpu.VMEM((16, 16, 640), BF),
            pltpu.VMEM((128, 640), BF),
            pltpu.SemaphoreType.DMA((4,)),
            *dma(3), *dma(7), *dma(7), *dma(7), *dma(1), *dma(4), *dma(16), *dma(8), *dma(16), *dma(8),
        ],
        compiler_params=pltpu.CompilerParams(
            collective_id=0, has_side_effects=True, vmem_limit_bytes=40 * 2**20
        ),
    )(*(pltpu.with_memory_space_constraint(v, pltpu.HBM) for v in (images, first_weight, deep_weight.T, deep_cotangent)))
    first, deep = pl.pallas_call(
        finish,
        out_shape=(jax.ShapeDtypeStruct((576, 128), F32), jax.ShapeDtypeStruct((32, 144), F32)),
        in_specs=[vmem, vmem],
        out_specs=(vmem, vmem),
        scratch_shapes=[pltpu.VMEM((256, 128), F32)],
        compiler_params=pltpu.CompilerParams(vmem_limit_bytes=40 * 2**20),
    )(first, deep)
    return first, deep.T


def solution(mesh):
    return jax.shard_map(
        on_device,
        mesh=mesh,
        in_specs=(P("sample", "row", "col"), P(), P(None, "col"), P("sample", "col", "row", None)),
        out_specs=(P(), P("row", "col")),
        check_vma=False,
    )
```

```python
import jax
import jax.numpy as jnp
from jax import lax
from jax.experimental import pallas as pl
from jax.experimental.pallas import tpu as pltpu
from jax.sharding import PartitionSpec as P

BF = jnp.bfloat16
F32 = jnp.float32
MESH = pl.DeviceIdType.MESH

HOPS = {(0, 0): 0, (0, 1): 1, (1, 1): 1, (1, 0): 2}
PLANE = sorted(
    ((dz, fx, fs) for dz in range(4) for fx in range(2) for fs in range(2) if dz + fx + fs),
    key=lambda step: -(min(step[0], 4 - step[0]) + HOPS[step[1:]]),
)
LINE = (4, 5, 3, 2, 6, 7, 1)
N_ROW = 8
N_COL = 8
N_BOTH = 16


def nn(a, b):
    return lax.dot_general(a, b, (((1,), (0,)), ((), ())), preferred_element_type=F32)


def nt(a, b):
    return lax.dot_general(a, b, (((1,), (1,)), ((), ())), preferred_element_type=F32)


def tn(a, b):
    return lax.dot_general(a, b, (((0,), (0,)), ((), ())), preferred_element_type=F32)


def eye(size):
    i = lax.broadcasted_iota(jnp.int32, (size, size), 0)
    j = lax.broadcasted_iota(jnp.int32, (size, size), 1)
    return (i == j).astype(F32).astype(BF)


def rows_of(index, size):
    return pl.ds(pl.multiple_of(index * size, size), size)


def remote(src, dst, send, recv, device):
    return pltpu.make_async_remote_copy(
        src_ref=src, dst_ref=dst, send_sem=send, recv_sem=recv, device_id=device, device_id_type=MESH
    )


class Fan:
    def __init__(self, pairs):
        self.pairs = list(pairs)

    def start(self):
        for out, _ in self.pairs:
            out.start()

    def wait_recv(self):
        for _, arriving in self.pairs:
            arriving.wait_recv()

    def wait_send(self):
        for out, _ in self.pairs:
            out.wait_send()


def kernel(
    img, w1, wd, cot, first_sum, deep_sum,
    xe, w1v, wdv, cotv, xr, w1f, wf, wdf, wt, cotf, cs, cr, q, acte, acto, sle, slo, patch,
    gw, pair_in, half, ra, gt, fa, sb, rb, sb2, rb2, gtall,
    in_sem, halo_s, halo_r, w_s, w_r, v_s, v_r, c_s, c_r, d0_s, d0_r, d1_s, d1_r, d2_s, d2_r,
    f1_s, f1_r, f2_s, f2_r, f3_s, f3_r,
):
    s, r, c = (lax.axis_index(name) for name in ("sample", "row", "col"))
    core = lax.rem(r, 2)
    partner = r + 1 - 2 * core
    plane = s * N_COL + c

    inputs = [
        pltpu.make_async_copy(cot.at[0], cotv, in_sem.at[0]),
        pltpu.make_async_copy(wd, wdv, in_sem.at[1]),
        pltpu.make_async_copy(w1, w1v, in_sem.at[2]),
        pltpu.make_async_copy(img.at[0], xe.at[pl.ds(16, 64), pl.ds(256, 4096)], in_sem.at[3]),
    ]

    z, xhi = c // 2, lax.rem(c, 2)

    def in_plane(step, sign=1):
        dz, fx, fs = step
        return lax.rem(s + fs, 2), lax.rem(z + 4 + sign * dz, 4) * 2 + lax.rem(xhi + fx, 2)

    down, right = lax.rem(r + 1, N_ROW), lax.rem(c + 1, N_COL)

    barrier = pltpu.get_barrier_semaphore()
    greeted = []
    for step in PLANE:
        ps, pc = in_plane(step)
        greeted.append((ps, r, pc))
    for k in LINE:
        greeted.append((s, lax.rem(r + k, N_ROW), c))
    for device in greeted:
        pl.semaphore_signal(barrier, inc=1, device_id=device, device_id_type=MESH)
    for copy in inputs:
        copy.start()

    unit = eye(128)

    inputs[0].wait()
    cotf[...] = cotv[...].reshape(512, 128).astype(F32)
    for g in range(4):
        picked = [cotf[pl.ds(4 * g + k, 32, stride=16), :] for k in range(4)]
        cs[g] = nt(unit, jnp.concatenate(picked, 0).astype(BF)).astype(BF)
    cr[0] = cs[:, rows_of(c, 16), :]

    inputs[1].wait()
    blank = jnp.zeros((96, 128), BF)
    for j in range(9):
        wdf[128 * j : 128 * j + 128] = nt(unit, jnp.concatenate([wdv[:, 128 * j : 128 * j + 128], blank], 0))
    for tap in range(9):
        piece = wdf[pl.ds(tap, 128, stride=9), :].astype(BF)
        wt[rows_of(c, 32), 128 * tap : 128 * tap + 128] = nt(unit, piece)[0:32].astype(BF)

    inputs[2].wait()
    w1f[...] = w1v[...].astype(F32)
    for ta in range(3):
        wf[ta, 0:64] = jnp.zeros((64, 128), BF)
        for tb in range(3):
            wf[ta, 64 * tb + 64 : 64 * tb + 128] = w1f[pl.ds(3 * ta + tb, 64, stride=9), :].astype(BF)

    pl.semaphore_wait(barrier, len(greeted))

    def halo(index, source, target, device):
        return remote(source, target, halo_s.at[index], halo_r.at[index], device)

    to_down = halo(0, img.at[0, pl.ds(48, 16), :], xe.at[pl.ds(0, 16), pl.ds(256, 4096)], (s, down, c))
    to_right = halo(1, img.at[0, :, pl.ds(3840, 256)], xe.at[pl.ds(16, 64), pl.ds(0, 256)], (s, r, right))
    to_corner = halo(2, xe.at[pl.ds(64, 16), pl.ds(0, 256)], xe.at[pl.ds(0, 16), pl.ds(0, 256)], (s, down, c))
    sends_down, sends_right = r < N_ROW - 1, c < N_COL - 1
    has_up, has_left = r > 0, c > 0

    @pl.when(sends_right)
    def _():
        to_right.start()

    def across(dz, dx, sign=1):
        return in_plane((dz, dx, dx), sign)

    def half_shard(col, which):
        return wt.at[pl.ds(pl.multiple_of(32 * col + 16 * which, 16), 16), :]

    far_first = ((2, 1), (1, 1), (3, 1), (2, 0), (1, 0), (3, 0), (0, 1))
    weights, handed_on = [], []
    for k, (dz, dx) in enumerate(far_first):
        ps, pc = across(dz, dx)
        qs, qc = across(dz, dx, -1)
        weights.append(
            (
                remote(half_shard(c, core), half_shard(c, core), w_s.at[k], w_r.at[k], (ps, r, pc)),
                remote(half_shard(qc, core), half_shard(qc, core), w_s.at[k], w_r.at[k], (qs, r, qc)),
            )
        )
        handed_on.append(
            (
                remote(half_shard(qc, core), half_shard(qc, core), v_s.at[k], v_r.at[k], (s, partner, c)),
                remote(half_shard(qc, 1 - core), half_shard(qc, 1 - core), v_s.at[k], v_r.at[k], (s, partner, c)),
            )
        )
    weights, handed_on = Fan(weights), Fan(handed_on)
    weights.start()

    @pl.when(sends_down)
    def _():
        to_down.start()

    cotangents = []
    for k, (dz, dx) in enumerate(far_first):
        _, pc = across(dz, dx)
        _, qc = across(dz, dx, -1)
        cotangents.append(
            (
                remote(cs.at[:, rows_of(pc, 16), :], cr.at[dz + 4 * dx], c_s.at[k], c_r.at[k], (s, r, pc)),
                remote(cs.at[:, rows_of(qc, 16), :], cr.at[dz + 4 * dx], c_s.at[k], c_r.at[k], (s, r, qc)),
            )
        )
    cotangents = Fan(cotangents)
    cotangents.start()

    @pl.when(jnp.logical_not(has_up))
    def _():
        xe[0:16, 256:4352] = jnp.zeros((16, 4096), BF)

    @pl.when(jnp.logical_not(has_left))
    def _():
        xe[16:80, 0:256] = jnp.zeros((64, 256), BF)

    @pl.when(jnp.logical_not(jnp.logical_and(has_up, has_left)))
    def _():
        xe[0:16, 0:256] = jnp.zeros((16, 256), BF)

    inputs[3].wait()

    @pl.when(has_up)
    def _():
        to_down.wait_recv()

    row = lax.broadcasted_iota(jnp.int32, (112, 80), 0)
    col = lax.broadcasted_iota(jnp.int32, (112, 80), 1)
    pick = (col == 13 + 4 * (row % 16) + row // 16).astype(F32).astype(BF)

    def select(t):
        xr[:, t] = nn(pick, xe[:, 256 * t : 256 * t + 256]).astype(BF).reshape(7, 16, 256)

    for t in range(1, 17):
        select(t)

    @pl.when(has_left)
    def _():
        to_right.wait_recv()

    @pl.when(jnp.logical_and(sends_down, has_left))
    def _():
        to_corner.start()

    for k in range(6, -1, -1):
        weights.pairs[k][1].wait_recv()
        handed_on.pairs[k][0].start()

    @pl.when(jnp.logical_and(has_up, has_left))
    def _():
        to_corner.wait_recv()

    select(0)

    def even_of(p):
        return xr[p].reshape(272, 256)

    def odd_of(p):
        return jnp.concatenate([xr[p, 0:16, :, 128:256], xr[p, 1:17, :, 0:128]], 2).reshape(256, 256)

    for a in range(3):
        even = nn(even_of(2 * a), wf[0]) + nn(even_of(2 * a + 1), wf[1]) + nn(even_of(2 * a + 2), wf[2])
        odd = nn(odd_of(2 * a), wf[0]) + nn(odd_of(2 * a + 1), wf[1]) + nn(odd_of(2 * a + 2), wf[2])
        for pre, act, slope, count in ((even, acte, sle, 17), (odd, acto, slo, 16)):
            sig = jax.nn.sigmoid(pre)
            act[a] = (pre * sig).astype(BF).reshape(count, 16, 128)
            slope[a] = (sig * (1.0 + pre * (1.0 - sig))).reshape(count, 16, 128)

    for a in range(3):
        patch[:, 384 * a : 384 * a + 128] = acte[a, 0:16].reshape(256, 128)
        patch[:, 384 * a + 128 : 384 * a + 256] = acto[a].reshape(256, 128)
        patch[:, 384 * a + 256 : 384 * a + 384] = acte[a, 1:17].reshape(256, 128)

    cotangents.wait_recv()
    quarter = lax.broadcasted_iota(jnp.int32, (16, 128), 1) // 32
    def from_col(col):
        return lax.rem(z + 4 - col // 2, 4) + 4 * lax.rem(xhi + col % 2, 2)

    for half_of in range(2):
        slots = [from_col(4 * half_of + i) for i in range(4)]
        for g in range(4):
            tiles = [cr[slots[i], g].astype(F32) for i in range(4)]
            for k in range(4):
                mixed = jnp.zeros((16, 128), F32)
                for i in range(4):
                    shift = (32 * (i - k)) % 128
                    moved = pltpu.roll(tiles[i], shift, 1) if shift else tiles[i]
                    mixed = jnp.where(quarter == i, moved, mixed)
                q[half_of, 16 * (4 * g + k) : 16 * (4 * g + k) + 16] = mixed
    cotangent = jnp.concatenate(
        [jnp.concatenate([q[h, pl.ds(n, 16, stride=16), :] for h in range(2)], 1) for n in range(16)], 0
    )

    handed_on.wait_recv()
    pre = nt(patch[...], wt[...])
    sig = jax.nn.sigmoid(pre)
    dg = (cotangent * (sig * (1.0 + pre * (1.0 - sig)))).astype(BF)

    back = nn(dg, wt[...])
    empty = jnp.zeros((1, 16, 128), F32)
    totals = [jnp.zeros((128, 256), F32) for _ in range(3)]
    for a in range(3):
        part = [back[:, 384 * a + 128 * b : 384 * a + 128 * b + 128].reshape(16, 16, 128) for b in range(3)]
        even = jnp.concatenate([part[0], empty], 0) + jnp.concatenate([empty, part[2]], 0)
        odd = part[1]
        if a == 1:
            even, odd = even.astype(BF).astype(F32), odd.astype(BF).astype(F32)
        even = (even * sle[a]).reshape(272, 128).astype(BF)
        odd = (odd * slo[a]).reshape(256, 128).astype(BF)
        for ta in range(3):
            totals[ta] += tn(even, even_of(2 * a + ta)) + tn(odd, odd_of(2 * a + ta))
    for ta in range(3):
        gt[:, 128 * ta : 128 * ta + 128] = totals[ta][:, 128:256].astype(BF)
    low = lax.broadcasted_iota(jnp.int32, (128, 128), 1) < 64
    both = jnp.where(low, pltpu.roll(totals[1][:, 0:128], 64, 1), totals[0][:, 0:128])
    gt[:, 384:512] = both.astype(BF)
    gt[:, 512:640] = totals[2][:, 0:128].astype(BF)

    first1 = []
    for k in LINE:
        pr, qr = lax.rem(r + k, N_ROW), lax.rem(r + N_ROW - k, N_ROW)
        first1.append(
            (
                remote(gt.at[rows_of(pr, 16), :], fa.at[k], f1_s.at[k], f1_r.at[k], (s, pr, c)),
                remote(gt.at[rows_of(qr, 16), :], fa.at[k], f1_s.at[k], f1_r.at[k], (s, qr, c)),
            )
        )
    first1 = Fan(first1)
    first1.start()

    gw[...] = tn(patch[...], dg).astype(BF).reshape(9, 4, 2, 16, 256)
    pair = remote(gw.at[:, :, 1 - core], pair_in, d0_s.at[0], d0_r.at[0], (s, partner, c))
    pair.start()
    pair.wait_recv()
    half[...] = (gw[:, :, core].astype(F32) + pair_in[...].astype(F32)).astype(BF)

    y = r // 2
    deep1 = []
    for k in (2, 1, 3):
        py, qy = lax.rem(y + k, 4), lax.rem(y + 4 - k, 4)
        deep1.append(
            (
                remote(half.at[:, py], ra.at[k], d1_s.at[k], d1_r.at[k], (s, 2 * py + core, c)),
                remote(half.at[:, qy], ra.at[k], d1_s.at[k], d1_r.at[k], (s, 2 * qy + core, c)),
            )
        )
    deep1 = Fan(deep1)
    deep1.start()

    first1.wait_recv()
    total = gt[rows_of(r, 16), :].astype(F32)
    for k in range(1, N_ROW):
        total = total + fa[k].astype(F32)
    sb2[...] = total.astype(BF)
    first2 = []
    for k, step in enumerate(PLANE):
        ps, pc = in_plane(step)
        qs, qc = in_plane(step, -1)
        first2.append(
            (
                remote(sb2, rb2.at[plane], f2_s.at[k], f2_r.at[k], (ps, r, pc)),
                remote(sb2, rb2.at[qs * N_COL + qc], f2_s.at[k], f2_r.at[k], (qs, r, qc)),
            )
        )
    first2 = Fan(first2)
    first2.start()
    rb2[plane] = sb2[...]

    deep1.wait_recv()
    total = half[:, y].astype(F32)
    for k in range(1, 4):
        total = total + ra[k].astype(F32)
    for h in range(2):
        block = total[0:8, :, 128 * h : 128 * h + 128].reshape(128, 128)
        sb[4 * h : 4 * h + 4, 0:2] = nt(unit, block.astype(BF)).astype(BF).reshape(4, 2, 16, 128)
        last = total[8, :, 128 * h : 128 * h + 128]
        for p in range(4):
            moved = pltpu.roll(last, 128 - 32 * p, 1) if p else last
            sb[4 * h + p, 2] = moved.astype(BF)
    deep2 = []
    for k, step in enumerate(PLANE):
        ps, pc = in_plane(step)
        qs, qc = in_plane(step, -1)
        deep2.append(
            (
                remote(sb.at[pc], rb.at[plane], d2_s.at[k], d2_r.at[k], (ps, r, pc)),
                remote(sb.at[qc], rb.at[qs * N_COL + qc], d2_s.at[k], d2_r.at[k], (qs, r, qc)),
            )
        )
    deep2 = Fan(deep2)
    deep2.start()
    rb[plane] = sb[c]

    first2.wait_recv()
    total = rb2[0].astype(F32)
    for p in range(1, N_BOTH):
        total = total + rb2[p].astype(F32)
    gtall[rows_of(r, 16), :] = total.astype(BF)
    first3 = []
    for k in LINE:
        pr, qr = lax.rem(r + k, N_ROW), lax.rem(r + N_ROW - k, N_ROW)
        first3.append(
            (
                remote(gtall.at[rows_of(r, 16), :], gtall.at[rows_of(r, 16), :], f3_s.at[k], f3_r.at[k], (s, pr, c)),
                remote(gtall.at[rows_of(qr, 16), :], gtall.at[rows_of(qr, 16), :], f3_s.at[k], f3_r.at[k], (s, qr, c)),
            )
        )
    first3 = Fan(first3)
    first3.start()

    deep2.wait_recv()
    total = rb[0].astype(F32)
    for p in range(1, N_BOTH):
        total = total + rb[p].astype(F32)
    deep_sum[...] = total

    first3.wait_recv()
    first_sum[...] = gtall[...]

    @pl.when(sends_down)
    def _():
        to_down.wait_send()

    @pl.when(sends_right)
    def _():
        to_right.wait_send()

    @pl.when(jnp.logical_and(sends_down, has_left))
    def _():
        to_corner.wait_send()

    pair.wait_send()
    for fan in (weights, handed_on, cotangents, first1, deep1, first2, deep2, first3):
        fan.wait_send()


def finish(first_sum, deep_sum, out1, out2, o2):
    unit = eye(128)
    places = ((0, 1), (0, 2), (1, 1), (1, 2), (2, 1), (2, 2), (1, 0), (0, 0), None, (2, 0))
    for j in range(5):
        block = nt(unit, first_sum[:, 128 * j : 128 * j + 128])
        for i in range(2):
            place = places[2 * j + i]
            if place is not None:
                out1[pl.ds(3 * place[0] + place[1], 64, stride=9), :] = block[64 * i : 64 * i + 64]
    most = jnp.concatenate([deep_sum[0], deep_sum[1], jnp.zeros((96, 128), F32)], 0).T
    for tap in range(9):
        o2[pl.ds(tap, 16, stride=9), :] = most[16 * tap : 16 * tap + 16] if tap < 8 else deep_sum[2]
    out2[...] = o2[...].T[0:32, 0:144]


def on_device(images, first_weight, deep_weight, deep_cotangent):
    anywhere = pl.BlockSpec(memory_space=pltpu.HBM)
    vmem = pl.BlockSpec(memory_space=pltpu.VMEM)

    def dma(count):
        return [pltpu.SemaphoreType.DMA((count,))] * 2

    first, deep = pl.pallas_call(
        kernel,
        out_shape=(jax.ShapeDtypeStruct((128, 640), BF), jax.ShapeDtypeStruct((3, 16, 128), F32)),
        in_specs=[anywhere] * 4,
        out_specs=(vmem, vmem),
        scratch_shapes=[
            pltpu.VMEM((80, 4352), BF),
            pltpu.VMEM((576, 128), BF),
            pltpu.VMEM((32, 1152), BF),
            pltpu.VMEM((32, 16, 128), BF),
            pltpu.VMEM((7, 17, 16, 256), BF),
            pltpu.VMEM((576, 128), F32),
            pltpu.VMEM((3, 256, 128), BF),
            pltpu.VMEM((1152, 128), F32),
            pltpu.VMEM((256, 1152), BF),
            pltpu.VMEM((512, 128), F32),
            pltpu.VMEM((4, 128, 128), BF),
            pltpu.VMEM((8, 4, 16, 128), BF),
            pltpu.VMEM((2, 256, 128), F32),
            pltpu.VMEM((3, 17, 16, 128), BF),
            pltpu.VMEM((3, 16, 16, 128), BF),
            pltpu.VMEM((3, 17, 16, 128), F32),
            pltpu.VMEM((3, 16, 16, 128), F32),
            pltpu.VMEM((256, 1152), BF),
            pltpu.VMEM((9, 4, 2, 16, 256), BF),
            pltpu.VMEM((9, 4, 16, 256), BF),
            pltpu.VMEM((9, 4, 16, 256), BF),
            pltpu.VMEM((4, 9, 16, 256), BF),
            pltpu.VMEM((128, 640), BF),
            pltpu.VMEM((8, 16, 640), BF),
            pltpu.VMEM((8, 3, 16, 128), BF),
            pltpu.VMEM((16, 3, 16, 128), BF),
            pltpu.VMEM((16, 640), BF),
            pltpu.VMEM((16, 16, 640), BF),
            pltpu.VMEM((128, 640), BF),
            pltpu.SemaphoreType.DMA((4,)),
            *dma(3), *dma(7), *dma(7), *dma(7), *dma(1), *dma(4), *dma(16), *dma(8), *dma(16), *dma(8),
        ],
        compiler_params=pltpu.CompilerParams(
            collective_id=0, has_side_effects=True, vmem_limit_bytes=40 * 2**20
        ),
    )(*(pltpu.with_memory_space_constraint(v, pltpu.HBM) for v in (images, first_weight, deep_weight.T, deep_cotangent)))
    first, deep = pl.pallas_call(
        finish,
        out_shape=(jax.ShapeDtypeStruct((576, 128), F32), jax.ShapeDtypeStruct((32, 144), F32)),
        in_specs=[vmem, vmem],
        out_specs=(vmem, vmem),
        scratch_shapes=[pltpu.VMEM((256, 128), F32)],
        compiler_params=pltpu.CompilerParams(vmem_limit_bytes=40 * 2**20),
    )(first, deep)
    return first, deep.T


def solution(mesh):
    return jax.shard_map(
        on_device,
        mesh=mesh,
        in_specs=(P("sample", "row", "col"), P(), P(None, "col"), P("sample", "col", "row", None)),
        out_specs=(P(), P("row", "col")),
        check_vma=False,
    )
```

```python
import jax
import jax.numpy as jnp
from jax import lax
from jax.experimental import pallas as pl
from jax.experimental.pallas import tpu as pltpu
from jax.sharding import PartitionSpec as P

BF = jnp.bfloat16
F32 = jnp.float32
MESH = pl.DeviceIdType.MESH

HOPS = {(0, 0): 0, (0, 1): 1, (1, 1): 1, (1, 0): 2}
PLANE = sorted(
    ((dz, fx, fs) for dz in range(4) for fx in range(2) for fs in range(2) if dz + fx + fs),
    key=lambda step: -(min(step[0], 4 - step[0]) + HOPS[step[1:]]),
)
LINE = (4, 5, 3, 2, 6, 7, 1)
N_ROW = 8
N_COL = 8
N_BOTH = 16


def nn(a, b):
    return lax.dot_general(a, b, (((1,), (0,)), ((), ())), preferred_element_type=F32)


def nt(a, b):
    return lax.dot_general(a, b, (((1,), (1,)), ((), ())), preferred_element_type=F32)


def tn(a, b):
    return lax.dot_general(a, b, (((0,), (0,)), ((), ())), preferred_element_type=F32)


def eye(size):
    i = lax.broadcasted_iota(jnp.int32, (size, size), 0)
    j = lax.broadcasted_iota(jnp.int32, (size, size), 1)
    return (i == j).astype(F32).astype(BF)


def rows_of(index, size):
    return pl.ds(pl.multiple_of(index * size, size), size)


def remote(src, dst, send, recv, device):
    return pltpu.make_async_remote_copy(
        src_ref=src, dst_ref=dst, send_sem=send, recv_sem=recv, device_id=device, device_id_type=MESH
    )


class Fan:
    def __init__(self, pairs):
        self.pairs = list(pairs)

    def start(self):
        for out, _ in self.pairs:
            out.start()

    def wait_recv(self):
        for _, arriving in self.pairs:
            arriving.wait_recv()

    def wait_send(self):
        for out, _ in self.pairs:
            out.wait_send()


def kernel(
    img, w1, wd, cot, first_sum, deep_sum,
    xe, w1v, wdv, cotv, xr, w1f, wf, wdf, wt, cotf, cs, cr, q, acte, acto, sle, slo, patch,
    gw, pair_in, half, ra, gt, fa, sb, rb, sb2, rb2, gtall,
    in_sem, halo_s, halo_r, w_s, w_r, v_s, v_r, c_s, c_r, d0_s, d0_r, d1_s, d1_r, d2_s, d2_r,
    f1_s, f1_r, f2_s, f2_r, f3_s, f3_r,
):
    s, r, c = (lax.axis_index(name) for name in ("sample", "row", "col"))
    core = lax.rem(r, 2)
    partner = r + 1 - 2 * core
    plane = s * N_COL + c

    inputs = [
        pltpu.make_async_copy(cot.at[0], cotv, in_sem.at[0]),
        pltpu.make_async_copy(wd, wdv, in_sem.at[1]),
        pltpu.make_async_copy(w1, w1v, in_sem.at[2]),
        pltpu.make_async_copy(img.at[0], xe.at[pl.ds(16, 64), pl.ds(256, 4096)], in_sem.at[3]),
    ]

    z, xhi = c // 2, lax.rem(c, 2)

    def in_plane(step, sign=1):
        dz, fx, fs = step
        return lax.rem(s + fs, 2), lax.rem(z + 4 + sign * dz, 4) * 2 + lax.rem(xhi + fx, 2)

    down, right = lax.rem(r + 1, N_ROW), lax.rem(c + 1, N_COL)

    barrier = pltpu.get_barrier_semaphore()
    greeted = []
    for step in PLANE:
        ps, pc = in_plane(step)
        greeted.append((ps, r, pc))
    for k in LINE:
        greeted.append((s, lax.rem(r + k, N_ROW), c))
    for device in greeted:
        pl.semaphore_signal(barrier, inc=1, device_id=device, device_id_type=MESH)
    for copy in inputs:
        copy.start()

    unit = eye(128)

    inputs[0].wait()
    cotf[...] = cotv[...].reshape(512, 128).astype(F32)
    for g in range(4):
        picked = [cotf[pl.ds(4 * g + k, 32, stride=16), :] for k in range(4)]
        cs[g] = nt(unit, jnp.concatenate(picked, 0).astype(BF)).astype(BF)
    cr[0] = cs[:, rows_of(c, 16), :]

    inputs[1].wait()
    blank = jnp.zeros((96, 128), BF)
    for j in range(9):
        wdf[128 * j : 128 * j + 128] = nt(unit, jnp.concatenate([wdv[:, 128 * j : 128 * j + 128], blank], 0))
    for tap in range(9):
        piece = wdf[pl.ds(tap, 128, stride=9), :].astype(BF)
        wt[rows_of(c, 32), 128 * tap : 128 * tap + 128] = nt(unit, piece)[0:32].astype(BF)

    inputs[2].wait()
    w1f[...] = w1v[...].astype(F32)
    for ta in range(3):
        wf[ta, 0:64] = jnp.zeros((64, 128), BF)
        for tb in range(3):
            wf[ta, 64 * tb + 64 : 64 * tb + 128] = w1f[pl.ds(3 * ta + tb, 64, stride=9), :].astype(BF)

    pl.semaphore_wait(barrier, len(greeted))

    def halo(index, source, target, device):
        return remote(source, target, halo_s.at[index], halo_r.at[index], device)

    to_down = halo(0, img.at[0, pl.ds(48, 16), :], xe.at[pl.ds(0, 16), pl.ds(256, 4096)], (s, down, c))
    to_right = halo(1, img.at[0, :, pl.ds(3840, 256)], xe.at[pl.ds(16, 64), pl.ds(0, 256)], (s, r, right))
    to_corner = halo(2, xe.at[pl.ds(64, 16), pl.ds(0, 256)], xe.at[pl.ds(0, 16), pl.ds(0, 256)], (s, down, c))
    sends_down, sends_right = r < N_ROW - 1, c < N_COL - 1
    has_up, has_left = r > 0, c > 0

    def across(dz, dx, sign=1):
        return in_plane((dz, dx, dx), sign)

    def half_shard(col, which):
        return wt.at[pl.ds(pl.multiple_of(32 * col + 16 * which, 16), 16), :]

    far_first = ((2, 1), (1, 1), (3, 1), (2, 0), (1, 0), (3, 0), (0, 1))
    weights, handed_on = [], []
    for k, (dz, dx) in enumerate(far_first):
        ps, pc = across(dz, dx)
        qs, qc = across(dz, dx, -1)
        weights.append(
            (
                remote(half_shard(c, core), half_shard(c, core), w_s.at[k], w_r.at[k], (ps, r, pc)),
                remote(half_shard(qc, core), half_shard(qc, core), w_s.at[k], w_r.at[k], (qs, r, qc)),
            )
        )
        handed_on.append(
            (
                remote(half_shard(qc, core), half_shard(qc, core), v_s.at[k], v_r.at[k], (s, partner, c)),
                remote(half_shard(qc, 1 - core), half_shard(qc, 1 - core), v_s.at[k], v_r.at[k], (s, partner, c)),
            )
        )
    weights, handed_on = Fan(weights), Fan(handed_on)
    weights.start()

    @pl.when(sends_right)
    def _():
        to_right.start()

    @pl.when(sends_down)
    def _():
        to_down.start()

    cotangents = []
    for k, (dz, dx) in enumerate(far_first):
        _, pc = across(dz, dx)
        _, qc = across(dz, dx, -1)
        cotangents.append(
            (
                remote(cs.at[:, rows_of(pc, 16), :], cr.at[dz + 4 * dx], c_s.at[k], c_r.at[k], (s, r, pc)),
                remote(cs.at[:, rows_of(qc, 16), :], cr.at[dz + 4 * dx], c_s.at[k], c_r.at[k], (s, r, qc)),
            )
        )
    cotangents = Fan(cotangents)

    @pl.when(jnp.logical_not(has_up))
    def _():
        xe[0:16, 256:4352] = jnp.zeros((16, 4096), BF)

    @pl.when(jnp.logical_not(has_left))
    def _():
        xe[16:80, 0:256] = jnp.zeros((64, 256), BF)

    @pl.when(jnp.logical_not(jnp.logical_and(has_up, has_left)))
    def _():
        xe[0:16, 0:256] = jnp.zeros((16, 256), BF)

    inputs[3].wait()

    @pl.when(has_up)
    def _():
        to_down.wait_recv()

    cotangents.start()
    row = lax.broadcasted_iota(jnp.int32, (112, 80), 0)
    col = lax.broadcasted_iota(jnp.int32, (112, 80), 1)
    pick = (col == 13 + 4 * (row % 16) + row // 16).astype(F32).astype(BF)

    def select(t):
        xr[:, t] = nn(pick, xe[:, 256 * t : 256 * t + 256]).astype(BF).reshape(7, 16, 256)

    for t in range(1, 17):
        select(t)

    @pl.when(has_left)
    def _():
        to_right.wait_recv()

    @pl.when(jnp.logical_and(sends_down, has_left))
    def _():
        to_corner.start()

    for k in range(6, -1, -1):
        weights.pairs[k][1].wait_recv()
        handed_on.pairs[k][0].start()

    @pl.when(jnp.logical_and(has_up, has_left))
    def _():
        to_corner.wait_recv()

    select(0)

    def even_of(p):
        return xr[p].reshape(272, 256)

    def odd_of(p):
        return jnp.concatenate([xr[p, 0:16, :, 128:256], xr[p, 1:17, :, 0:128]], 2).reshape(256, 256)

    for a in range(3):
        even = nn(even_of(2 * a), wf[0]) + nn(even_of(2 * a + 1), wf[1]) + nn(even_of(2 * a + 2), wf[2])
        odd = nn(odd_of(2 * a), wf[0]) + nn(odd_of(2 * a + 1), wf[1]) + nn(odd_of(2 * a + 2), wf[2])
        for pre, act, slope, count in ((even, acte, sle, 17), (odd, acto, slo, 16)):
            sig = jax.nn.sigmoid(pre)
            act[a] = (pre * sig).astype(BF).reshape(count, 16, 128)
            slope[a] = (sig * (1.0 + pre * (1.0 - sig))).reshape(count, 16, 128)

    for a in range(3):
        patch[:, 384 * a : 384 * a + 128] = acte[a, 0:16].reshape(256, 128)
        patch[:, 384 * a + 128 : 384 * a + 256] = acto[a].reshape(256, 128)
        patch[:, 384 * a + 256 : 384 * a + 384] = acte[a, 1:17].reshape(256, 128)

    cotangents.wait_recv()
    quarter = lax.broadcasted_iota(jnp.int32, (16, 128), 1) // 32
    def from_col(col):
        return lax.rem(z + 4 - col // 2, 4) + 4 * lax.rem(xhi + col % 2, 2)

    for half_of in range(2):
        slots = [from_col(4 * half_of + i) for i in range(4)]
        for g in range(4):
            tiles = [cr[slots[i], g].astype(F32) for i in range(4)]
            for k in range(4):
                mixed = jnp.zeros((16, 128), F32)
                for i in range(4):
                    shift = (32 * (i - k)) % 128
                    moved = pltpu.roll(tiles[i], shift, 1) if shift else tiles[i]
                    mixed = jnp.where(quarter == i, moved, mixed)
                q[half_of, 16 * (4 * g + k) : 16 * (4 * g + k) + 16] = mixed
    cotangent = jnp.concatenate(
        [jnp.concatenate([q[h, pl.ds(n, 16, stride=16), :] for h in range(2)], 1) for n in range(16)], 0
    )

    handed_on.wait_recv()
    pre = nt(patch[...], wt[...])
    sig = jax.nn.sigmoid(pre)
    dg = (cotangent * (sig * (1.0 + pre * (1.0 - sig)))).astype(BF)

    back = nn(dg, wt[...])
    empty = jnp.zeros((1, 16, 128), F32)
    totals = [jnp.zeros((128, 256), F32) for _ in range(3)]
    for a in range(3):
        part = [back[:, 384 * a + 128 * b : 384 * a + 128 * b + 128].reshape(16, 16, 128) for b in range(3)]
        even = jnp.concatenate([part[0], empty], 0) + jnp.concatenate([empty, part[2]], 0)
        odd = part[1]
        if a == 1:
            even, odd = even.astype(BF).astype(F32), odd.astype(BF).astype(F32)
        even = (even * sle[a]).reshape(272, 128).astype(BF)
        odd = (odd * slo[a]).reshape(256, 128).astype(BF)
        for ta in range(3):
            totals[ta] += tn(even, even_of(2 * a + ta)) + tn(odd, odd_of(2 * a + ta))
    for ta in range(3):
        gt[:, 128 * ta : 128 * ta + 128] = totals[ta][:, 128:256].astype(BF)
    low = lax.broadcasted_iota(jnp.int32, (128, 128), 1) < 64
    both = jnp.where(low, pltpu.roll(totals[1][:, 0:128], 64, 1), totals[0][:, 0:128])
    gt[:, 384:512] = both.astype(BF)
    gt[:, 512:640] = totals[2][:, 0:128].astype(BF)

    first1 = []
    for k in LINE:
        pr, qr = lax.rem(r + k, N_ROW), lax.rem(r + N_ROW - k, N_ROW)
        first1.append(
            (
                remote(gt.at[rows_of(pr, 16), :], fa.at[k], f1_s.at[k], f1_r.at[k], (s, pr, c)),
                remote(gt.at[rows_of(qr, 16), :], fa.at[k], f1_s.at[k], f1_r.at[k], (s, qr, c)),
            )
        )
    first1 = Fan(first1)
    first1.start()

    gw[...] = tn(patch[...], dg).astype(BF).reshape(9, 4, 2, 16, 256)
    pair = remote(gw.at[:, :, 1 - core], pair_in, d0_s.at[0], d0_r.at[0], (s, partner, c))
    pair.start()
    pair.wait_recv()
    half[...] = (gw[:, :, core].astype(F32) + pair_in[...].astype(F32)).astype(BF)

    y = r // 2
    deep1 = []
    for k in (2, 1, 3):
        py, qy = lax.rem(y + k, 4), lax.rem(y + 4 - k, 4)
        deep1.append(
            (
                remote(half.at[:, py], ra.at[k], d1_s.at[k], d1_r.at[k], (s, 2 * py + core, c)),
                remote(half.at[:, qy], ra.at[k], d1_s.at[k], d1_r.at[k], (s, 2 * qy + core, c)),
            )
        )
    deep1 = Fan(deep1)
    deep1.start()

    first1.wait_recv()
    total = gt[rows_of(r, 16), :].astype(F32)
    for k in range(1, N_ROW):
        total = total + fa[k].astype(F32)
    sb2[...] = total.astype(BF)
    first2 = []
    for k, step in enumerate(PLANE):
        ps, pc = in_plane(step)
        qs, qc = in_plane(step, -1)
        first2.append(
            (
                remote(sb2, rb2.at[plane], f2_s.at[k], f2_r.at[k], (ps, r, pc)),
                remote(sb2, rb2.at[qs * N_COL + qc], f2_s.at[k], f2_r.at[k], (qs, r, qc)),
            )
        )
    first2 = Fan(first2)
    first2.start()
    rb2[plane] = sb2[...]

    deep1.wait_recv()
    total = half[:, y].astype(F32)
    for k in range(1, 4):
        total = total + ra[k].astype(F32)
    for h in range(2):
        block = total[0:8, :, 128 * h : 128 * h + 128].reshape(128, 128)
        sb[4 * h : 4 * h + 4, 0:2] = nt(unit, block.astype(BF)).astype(BF).reshape(4, 2, 16, 128)
        last = total[8, :, 128 * h : 128 * h + 128]
        for p in range(4):
            moved = pltpu.roll(last, 128 - 32 * p, 1) if p else last
            sb[4 * h + p, 2] = moved.astype(BF)
    deep2 = []
    for k, step in enumerate(PLANE):
        ps, pc = in_plane(step)
        qs, qc = in_plane(step, -1)
        deep2.append(
            (
                remote(sb.at[pc], rb.at[plane], d2_s.at[k], d2_r.at[k], (ps, r, pc)),
                remote(sb.at[qc], rb.at[qs * N_COL + qc], d2_s.at[k], d2_r.at[k], (qs, r, qc)),
            )
        )
    deep2 = Fan(deep2)
    deep2.start()
    rb[plane] = sb[c]

    @pl.when(sends_down)
    def _():
        to_down.wait_send()

    @pl.when(sends_right)
    def _():
        to_right.wait_send()

    @pl.when(jnp.logical_and(sends_down, has_left))
    def _():
        to_corner.wait_send()

    pair.wait_send()
    for fan in (weights, handed_on, cotangents, first1, deep1):
        fan.wait_send()

    first2.wait_recv()
    total = rb2[0].astype(F32)
    for p in range(1, N_BOTH):
        total = total + rb2[p].astype(F32)
    gtall[rows_of(r, 16), :] = total.astype(BF)
    first3 = []
    for k in LINE:
        pr, qr = lax.rem(r + k, N_ROW), lax.rem(r + N_ROW - k, N_ROW)
        first3.append(
            (
                remote(gtall.at[rows_of(r, 16), :], gtall.at[rows_of(r, 16), :], f3_s.at[k], f3_r.at[k], (s, pr, c)),
                remote(gtall.at[rows_of(qr, 16), :], gtall.at[rows_of(qr, 16), :], f3_s.at[k], f3_r.at[k], (s, qr, c)),
            )
        )
    first3 = Fan(first3)
    first3.start()

    deep2.wait_recv()
    total = rb[0].astype(F32)
    for p in range(1, N_BOTH):
        total = total + rb[p].astype(F32)
    deep_sum[...] = total

    for fan in (first2, deep2):
        fan.wait_send()
    first3.wait_recv()
    first_sum[...] = gtall[...]

    first3.wait_send()


def finish(first_sum, deep_sum, out1, out2, o2):
    unit = eye(128)
    places = ((0, 1), (0, 2), (1, 1), (1, 2), (2, 1), (2, 2), (1, 0), (0, 0), None, (2, 0))
    for j in range(5):
        block = nt(unit, first_sum[:, 128 * j : 128 * j + 128])
        for i in range(2):
            place = places[2 * j + i]
            if place is not None:
                out1[pl.ds(3 * place[0] + place[1], 64, stride=9), :] = block[64 * i : 64 * i + 64]
    most = jnp.concatenate([deep_sum[0], deep_sum[1], jnp.zeros((96, 128), F32)], 0).T
    for tap in range(9):
        o2[pl.ds(tap, 16, stride=9), :] = most[16 * tap : 16 * tap + 16] if tap < 8 else deep_sum[2]
    out2[...] = o2[...].T[0:32, 0:144]


def on_device(images, first_weight, deep_weight, deep_cotangent):
    anywhere = pl.BlockSpec(memory_space=pltpu.HBM)
    vmem = pl.BlockSpec(memory_space=pltpu.VMEM)

    def dma(count):
        return [pltpu.SemaphoreType.DMA((count,))] * 2

    first, deep = pl.pallas_call(
        kernel,
        out_shape=(jax.ShapeDtypeStruct((128, 640), BF), jax.ShapeDtypeStruct((3, 16, 128), F32)),
        in_specs=[anywhere] * 4,
        out_specs=(vmem, vmem),
        scratch_shapes=[
            pltpu.VMEM((80, 4352), BF),
            pltpu.VMEM((576, 128), BF),
            pltpu.VMEM((32, 1152), BF),
            pltpu.VMEM((32, 16, 128), BF),
            pltpu.VMEM((7, 17, 16, 256), BF),
            pltpu.VMEM((576, 128), F32),
            pltpu.VMEM((3, 256, 128), BF),
            pltpu.VMEM((1152, 128), F32),
            pltpu.VMEM((256, 1152), BF),
            pltpu.VMEM((512, 128), F32),
            pltpu.VMEM((4, 128, 128), BF),
            pltpu.VMEM((8, 4, 16, 128), BF),
            pltpu.VMEM((2, 256, 128), F32),
            pltpu.VMEM((3, 17, 16, 128), BF),
            pltpu.VMEM((3, 16, 16, 128), BF),
            pltpu.VMEM((3, 17, 16, 128), F32),
            pltpu.VMEM((3, 16, 16, 128), F32),
            pltpu.VMEM((256, 1152), BF),
            pltpu.VMEM((9, 4, 2, 16, 256), BF),
            pltpu.VMEM((9, 4, 16, 256), BF),
            pltpu.VMEM((9, 4, 16, 256), BF),
            pltpu.VMEM((4, 9, 16, 256), BF),
            pltpu.VMEM((128, 640), BF),
            pltpu.VMEM((8, 16, 640), BF),
            pltpu.VMEM((8, 3, 16, 128), BF),
            pltpu.VMEM((16, 3, 16, 128), BF),
            pltpu.VMEM((16, 640), BF),
            pltpu.VMEM((16, 16, 640), BF),
            pltpu.VMEM((128, 640), BF),
            pltpu.SemaphoreType.DMA((4,)),
            *dma(3), *dma(7), *dma(7), *dma(7), *dma(1), *dma(4), *dma(16), *dma(8), *dma(16), *dma(8),
        ],
        compiler_params=pltpu.CompilerParams(
            collective_id=0, has_side_effects=True, vmem_limit_bytes=40 * 2**20
        ),
    )(*(pltpu.with_memory_space_constraint(v, pltpu.HBM) for v in (images, first_weight, deep_weight.T, deep_cotangent)))
    first, deep = pl.pallas_call(
        finish,
        out_shape=(jax.ShapeDtypeStruct((576, 128), F32), jax.ShapeDtypeStruct((32, 144), F32)),
        in_specs=[vmem, vmem],
        out_specs=(vmem, vmem),
        scratch_shapes=[pltpu.VMEM((256, 128), F32)],
        compiler_params=pltpu.CompilerParams(vmem_limit_bytes=40 * 2**20),
    )(first, deep)
    return first, deep.T


def solution(mesh):
    return jax.shard_map(
        on_device,
        mesh=mesh,
        in_specs=(P("sample", "row", "col"), P(), P(None, "col"), P("sample", "col", "row", None)),
        out_specs=(P(), P("row", "col")),
        check_vma=False,
    )
```

```python
import jax
import jax.numpy as jnp
from jax import lax
from jax.experimental import pallas as pl
from jax.experimental.pallas import tpu as pltpu
from jax.sharding import PartitionSpec as P

BF = jnp.bfloat16
F32 = jnp.float32
MESH = pl.DeviceIdType.MESH

HOPS = {(0, 0): 0, (0, 1): 1, (1, 1): 1, (1, 0): 2}
PLANE = sorted(
    ((dz, fx, fs) for dz in range(4) for fx in range(2) for fs in range(2) if dz + fx + fs),
    key=lambda step: -(min(step[0], 4 - step[0]) + HOPS[step[1:]]),
)
LINE = (4, 5, 3, 2, 6, 7, 1)
N_ROW = 8
N_COL = 8
N_BOTH = 16


def nn(a, b):
    return lax.dot_general(a, b, (((1,), (0,)), ((), ())), preferred_element_type=F32)


def nt(a, b):
    return lax.dot_general(a, b, (((1,), (1,)), ((), ())), preferred_element_type=F32)


def tn(a, b):
    return lax.dot_general(a, b, (((0,), (0,)), ((), ())), preferred_element_type=F32)


def eye(size):
    i = lax.broadcasted_iota(jnp.int32, (size, size), 0)
    j = lax.broadcasted_iota(jnp.int32, (size, size), 1)
    return (i == j).astype(F32).astype(BF)


def rows_of(index, size):
    return pl.ds(pl.multiple_of(index * size, size), size)


def remote(src, dst, send, recv, device):
    return pltpu.make_async_remote_copy(
        src_ref=src, dst_ref=dst, send_sem=send, recv_sem=recv, device_id=device, device_id_type=MESH
    )


class Fan:
    def __init__(self, pairs):
        self.pairs = list(pairs)

    def start(self):
        for out, _ in self.pairs:
            out.start()

    def wait_recv(self):
        for _, arriving in self.pairs:
            arriving.wait_recv()

    def wait_send(self):
        for out, _ in self.pairs:
            out.wait_send()


def kernel(
    img, w1, wd, cot, first_sum, deep_sum,
    xe, w1v, wdv, cotv, xr, w1f, wf, wdf, wt, cotf, cs, cr, q, acte, acto, sle, slo, patch,
    gw, pair_in, half, ra, gt, fa, sb, rb, sb2, rb2, gtall, o2,
    in_sem, halo_s, halo_r, w_s, w_r, v_s, v_r, c_s, c_r, d0_s, d0_r, d1_s, d1_r, d2_s, d2_r,
    f1_s, f1_r, f2_s, f2_r, f3_s, f3_r,
):
    s, r, c = (lax.axis_index(name) for name in ("sample", "row", "col"))
    core = lax.rem(r, 2)
    partner = r + 1 - 2 * core
    plane = s * N_COL + c

    inputs = [
        pltpu.make_async_copy(cot.at[0], cotv, in_sem.at[0]),
        pltpu.make_async_copy(wd, wdv, in_sem.at[1]),
        pltpu.make_async_copy(w1, w1v, in_sem.at[2]),
        pltpu.make_async_copy(img.at[0], xe.at[pl.ds(16, 64), pl.ds(256, 4096)], in_sem.at[3]),
    ]

    z, xhi = c // 2, lax.rem(c, 2)

    def in_plane(step, sign=1):
        dz, fx, fs = step
        return lax.rem(s + fs, 2), lax.rem(z + 4 + sign * dz, 4) * 2 + lax.rem(xhi + fx, 2)

    down, right = lax.rem(r + 1, N_ROW), lax.rem(c + 1, N_COL)

    barrier = pltpu.get_barrier_semaphore()
    greeted = []
    for step in PLANE:
        ps, pc = in_plane(step)
        greeted.append((ps, r, pc))
    for k in LINE:
        greeted.append((s, lax.rem(r + k, N_ROW), c))
    for device in greeted:
        pl.semaphore_signal(barrier, inc=1, device_id=device, device_id_type=MESH)
    for copy in inputs:
        copy.start()

    unit = eye(128)

    inputs[0].wait()
    cotf[...] = cotv[...].reshape(512, 128).astype(F32)
    for g in range(4):
        picked = [cotf[pl.ds(4 * g + k, 32, stride=16), :] for k in range(4)]
        cs[g] = nt(unit, jnp.concatenate(picked, 0).astype(BF)).astype(BF)
    cr[0] = cs[:, rows_of(c, 16), :]

    inputs[1].wait()
    blank = jnp.zeros((96, 128), BF)
    for j in range(9):
        wdf[128 * j : 128 * j + 128] = nt(unit, jnp.concatenate([wdv[:, 128 * j : 128 * j + 128], blank], 0))
    for tap in range(9):
        piece = wdf[pl.ds(tap, 128, stride=9), :].astype(BF)
        wt[rows_of(c, 32), 128 * tap : 128 * tap + 128] = nt(unit, piece)[0:32].astype(BF)

    inputs[2].wait()
    w1f[...] = w1v[...].astype(F32)
    for ta in range(3):
        wf[ta, 0:64] = jnp.zeros((64, 128), BF)
        for tb in range(3):
            wf[ta, 64 * tb + 64 : 64 * tb + 128] = w1f[pl.ds(3 * ta + tb, 64, stride=9), :].astype(BF)

    pl.semaphore_wait(barrier, len(greeted))

    def halo(index, source, target, device):
        return remote(source, target, halo_s.at[index], halo_r.at[index], device)

    to_down = halo(0, img.at[0, pl.ds(48, 16), :], xe.at[pl.ds(0, 16), pl.ds(256, 4096)], (s, down, c))
    to_right = halo(1, img.at[0, :, pl.ds(3840, 256)], xe.at[pl.ds(16, 64), pl.ds(0, 256)], (s, r, right))
    to_corner = halo(2, xe.at[pl.ds(64, 16), pl.ds(0, 256)], xe.at[pl.ds(0, 16), pl.ds(0, 256)], (s, down, c))
    sends_down, sends_right = r < N_ROW - 1, c < N_COL - 1
    has_up, has_left = r > 0, c > 0

    def across(dz, dx, sign=1):
        return in_plane((dz, dx, dx), sign)

    def half_shard(col, which):
        return wt.at[pl.ds(pl.multiple_of(32 * col + 16 * which, 16), 16), :]

    far_first = ((2, 1), (1, 1), (3, 1), (2, 0), (1, 0), (3, 0), (0, 1))
    weights, handed_on = [], []
    for k, (dz, dx) in enumerate(far_first):
        ps, pc = across(dz, dx)
        qs, qc = across(dz, dx, -1)
        weights.append(
            (
                remote(half_shard(c, core), half_shard(c, core), w_s.at[k], w_r.at[k], (ps, r, pc)),
                remote(half_shard(qc, core), half_shard(qc, core), w_s.at[k], w_r.at[k], (qs, r, qc)),
            )
        )
        handed_on.append(
            (
                remote(half_shard(qc, core), half_shard(qc, core), v_s.at[k], v_r.at[k], (s, partner, c)),
                remote(half_shard(qc, 1 - core), half_shard(qc, 1 - core), v_s.at[k], v_r.at[k], (s, partner, c)),
            )
        )
    weights, handed_on = Fan(weights), Fan(handed_on)
    weights.start()

    @pl.when(sends_right)
    def _():
        to_right.start()

    @pl.when(sends_down)
    def _():
        to_down.start()

    cotangents = []
    for k, (dz, dx) in enumerate(far_first):
        _, pc = across(dz, dx)
        _, qc = across(dz, dx, -1)
        cotangents.append(
            (
                remote(cs.at[:, rows_of(pc, 16), :], cr.at[dz + 4 * dx], c_s.at[k], c_r.at[k], (s, r, pc)),
                remote(cs.at[:, rows_of(qc, 16), :], cr.at[dz + 4 * dx], c_s.at[k], c_r.at[k], (s, r, qc)),
            )
        )
    cotangents = Fan(cotangents)

    @pl.when(jnp.logical_not(has_up))
    def _():
        xe[0:16, 256:4352] = jnp.zeros((16, 4096), BF)

    @pl.when(jnp.logical_not(has_left))
    def _():
        xe[16:80, 0:256] = jnp.zeros((64, 256), BF)

    @pl.when(jnp.logical_not(jnp.logical_and(has_up, has_left)))
    def _():
        xe[0:16, 0:256] = jnp.zeros((16, 256), BF)

    inputs[3].wait()

    @pl.when(has_up)
    def _():
        to_down.wait_recv()

    cotangents.start()
    row = lax.broadcasted_iota(jnp.int32, (112, 80), 0)
    col = lax.broadcasted_iota(jnp.int32, (112, 80), 1)
    pick = (col == 13 + 4 * (row % 16) + row // 16).astype(F32).astype(BF)

    def select(t):
        xr[:, t] = nn(pick, xe[:, 256 * t : 256 * t + 256]).astype(BF).reshape(7, 16, 256)

    for t in range(1, 17):
        select(t)

    @pl.when(has_left)
    def _():
        to_right.wait_recv()

    @pl.when(jnp.logical_and(sends_down, has_left))
    def _():
        to_corner.start()

    for k in range(6, -1, -1):
        weights.pairs[k][1].wait_recv()
        handed_on.pairs[k][0].start()

    @pl.when(jnp.logical_and(has_up, has_left))
    def _():
        to_corner.wait_recv()

    select(0)

    def even_of(p):
        return xr[p].reshape(272, 256)

    def odd_of(p):
        return jnp.concatenate([xr[p, 0:16, :, 128:256], xr[p, 1:17, :, 0:128]], 2).reshape(256, 256)

    for a in range(3):
        even = nn(even_of(2 * a), wf[0]) + nn(even_of(2 * a + 1), wf[1]) + nn(even_of(2 * a + 2), wf[2])
        odd = nn(odd_of(2 * a), wf[0]) + nn(odd_of(2 * a + 1), wf[1]) + nn(odd_of(2 * a + 2), wf[2])
        for pre, act, slope, count in ((even, acte, sle, 17), (odd, acto, slo, 16)):
            sig = jax.nn.sigmoid(pre)
            act[a] = (pre * sig).astype(BF).reshape(count, 16, 128)
            slope[a] = (sig * (1.0 + pre * (1.0 - sig))).reshape(count, 16, 128)

    for a in range(3):
        patch[:, 384 * a : 384 * a + 128] = acte[a, 0:16].reshape(256, 128)
        patch[:, 384 * a + 128 : 384 * a + 256] = acto[a].reshape(256, 128)
        patch[:, 384 * a + 256 : 384 * a + 384] = acte[a, 1:17].reshape(256, 128)

    cotangents.wait_recv()
    quarter = lax.broadcasted_iota(jnp.int32, (16, 128), 1) // 32
    def from_col(col):
        return lax.rem(z + 4 - col // 2, 4) + 4 * lax.rem(xhi + col % 2, 2)

    for half_of in range(2):
        slots = [from_col(4 * half_of + i) for i in range(4)]
        for g in range(4):
            tiles = [cr[slots[i], g].astype(F32) for i in range(4)]
            for k in range(4):
                mixed = jnp.zeros((16, 128), F32)
                for i in range(4):
                    shift = (32 * (i - k)) % 128
                    moved = pltpu.roll(tiles[i], shift, 1) if shift else tiles[i]
                    mixed = jnp.where(quarter == i, moved, mixed)
                q[half_of, 16 * (4 * g + k) : 16 * (4 * g + k) + 16] = mixed
    cotangent = jnp.concatenate(
        [jnp.concatenate([q[h, pl.ds(n, 16, stride=16), :] for h in range(2)], 1) for n in range(16)], 0
    )

    handed_on.wait_recv()
    pre = nt(patch[...], wt[...])
    sig = jax.nn.sigmoid(pre)
    dg = (cotangent * (sig * (1.0 + pre * (1.0 - sig)))).astype(BF)

    back = nn(dg, wt[...])
    empty = jnp.zeros((1, 16, 128), F32)
    totals = [jnp.zeros((128, 256), F32) for _ in range(3)]
    edge = []
    for a in range(3):
        part = [back[:, 384 * a + 128 * b : 384 * a + 128 * b + 128].reshape(16, 16, 128) for b in range(3)]
        even = jnp.concatenate([part[0], empty], 0) + jnp.concatenate([empty, part[2]], 0)
        odd = part[1]
        if a == 1:
            even, odd = even.astype(BF).astype(F32), odd.astype(BF).astype(F32)
        even = (even * sle[a]).reshape(272, 128).astype(BF)
        odd = (odd * slo[a]).reshape(256, 128).astype(BF)
        edge.append(even[0:16])
        for ta in range(3):
            inner = xr[2 * a + ta, 1:17].reshape(256, 256)
            totals[ta] += tn(even[16:272], inner) + tn(odd, odd_of(2 * a + ta))
    edge = jnp.concatenate(edge, 0)
    for ta in range(3):
        totals[ta] += tn(edge, jnp.concatenate([xr[2 * a + ta, 0] for a in range(3)], 0))
    for ta in range(3):
        gt[:, 128 * ta : 128 * ta + 128] = totals[ta][:, 128:256].astype(BF)
    low = lax.broadcasted_iota(jnp.int32, (128, 128), 1) < 64
    both = jnp.where(low, pltpu.roll(totals[1][:, 0:128], 64, 1), totals[0][:, 0:128])
    gt[:, 384:512] = both.astype(BF)
    gt[:, 512:640] = totals[2][:, 0:128].astype(BF)

    first1 = []
    for k in LINE:
        pr, qr = lax.rem(r + k, N_ROW), lax.rem(r + N_ROW - k, N_ROW)
        first1.append(
            (
                remote(gt.at[rows_of(pr, 16), :], fa.at[k], f1_s.at[k], f1_r.at[k], (s, pr, c)),
                remote(gt.at[rows_of(qr, 16), :], fa.at[k], f1_s.at[k], f1_r.at[k], (s, qr, c)),
            )
        )
    first1 = Fan(first1)
    first1.start()

    gw[...] = tn(patch[...], dg).astype(BF).reshape(9, 4, 2, 16, 256)
    pair = remote(gw.at[:, :, 1 - core], pair_in, d0_s.at[0], d0_r.at[0], (s, partner, c))
    pair.start()
    pair.wait_recv()
    half[...] = (gw[:, :, core].astype(F32) + pair_in[...].astype(F32)).astype(BF)

    y = r // 2
    deep1 = []
    for k in (2, 1, 3):
        py, qy = lax.rem(y + k, 4), lax.rem(y + 4 - k, 4)
        deep1.append(
            (
                remote(half.at[:, py], ra.at[k], d1_s.at[k], d1_r.at[k], (s, 2 * py + core, c)),
                remote(half.at[:, qy], ra.at[k], d1_s.at[k], d1_r.at[k], (s, 2 * qy + core, c)),
            )
        )
    deep1 = Fan(deep1)

    first1.wait_recv()
    total = gt[rows_of(r, 16), :].astype(F32)
    for k in range(1, N_ROW):
        total = total + fa[k].astype(F32)
    sb2[...] = total.astype(BF)
    first2 = []
    for k, step in enumerate(PLANE):
        ps, pc = in_plane(step)
        qs, qc = in_plane(step, -1)
        first2.append(
            (
                remote(sb2, rb2.at[plane], f2_s.at[k], f2_r.at[k], (ps, r, pc)),
                remote(sb2, rb2.at[qs * N_COL + qc], f2_s.at[k], f2_r.at[k], (qs, r, qc)),
            )
        )
    first2 = Fan(first2)
    first2.start()
    deep1.start()
    rb2[plane] = sb2[...]

    deep1.wait_recv()
    total = half[:, y].astype(F32)
    for k in range(1, 4):
        total = total + ra[k].astype(F32)
    for h in range(2):
        block = total[0:8, :, 128 * h : 128 * h + 128].reshape(128, 128)
        sb[4 * h : 4 * h + 4, 0:2] = nt(unit, block.astype(BF)).astype(BF).reshape(4, 2, 16, 128)
        last = total[8, :, 128 * h : 128 * h + 128]
        for p in range(4):
            moved = pltpu.roll(last, 128 - 32 * p, 1) if p else last
            sb[4 * h + p, 2] = moved.astype(BF)
    deep2 = []
    for k, step in enumerate(PLANE):
        ps, pc = in_plane(step)
        qs, qc = in_plane(step, -1)
        deep2.append(
            (
                remote(sb.at[pc], rb.at[plane], d2_s.at[k], d2_r.at[k], (ps, r, pc)),
                remote(sb.at[qc], rb.at[qs * N_COL + qc], d2_s.at[k], d2_r.at[k], (qs, r, qc)),
            )
        )
    deep2 = Fan(deep2)
    deep2.start()
    rb[plane] = sb[c]

    @pl.when(sends_down)
    def _():
        to_down.wait_send()

    @pl.when(sends_right)
    def _():
        to_right.wait_send()

    @pl.when(jnp.logical_and(sends_down, has_left))
    def _():
        to_corner.wait_send()

    pair.wait_send()
    for fan in (weights, handed_on, cotangents, first1, deep1):
        fan.wait_send()

    first2.wait_recv()
    total = rb2[0].astype(F32)
    for p in range(1, N_BOTH):
        total = total + rb2[p].astype(F32)
    gtall[rows_of(r, 16), :] = total.astype(BF)
    first3 = []
    for k in LINE:
        pr, qr = lax.rem(r + k, N_ROW), lax.rem(r + N_ROW - k, N_ROW)
        first3.append(
            (
                remote(gtall.at[rows_of(r, 16), :], gtall.at[rows_of(r, 16), :], f3_s.at[k], f3_r.at[k], (s, pr, c)),
                remote(gtall.at[rows_of(qr, 16), :], gtall.at[rows_of(qr, 16), :], f3_s.at[k], f3_r.at[k], (s, qr, c)),
            )
        )
    first3 = Fan(first3)
    first3.start()

    deep2.wait_recv()
    total = rb[0].astype(F32)
    for p in range(1, N_BOTH):
        total = total + rb[p].astype(F32)
    most = jnp.concatenate([total[0], total[1], jnp.zeros((96, 128), F32)], 0).T
    for tap in range(9):
        o2[pl.ds(tap, 16, stride=9), :] = most[16 * tap : 16 * tap + 16] if tap < 8 else total[2]
    deep_sum[...] = o2[...].T[0:32, 0:144]

    for fan in (first2, deep2):
        fan.wait_send()
    first3.wait_recv()
    first_sum[...] = gtall[...]

    first3.wait_send()


def finish(first_sum, deep_sum, out1, out2):
    unit = eye(128)
    places = ((0, 1), (0, 2), (1, 1), (1, 2), (2, 1), (2, 2), (1, 0), (0, 0), None, (2, 0))
    for j in range(5):
        block = nt(unit, first_sum[:, 128 * j : 128 * j + 128])
        for i in range(2):
            place = places[2 * j + i]
            if place is not None:
                out1[pl.ds(3 * place[0] + place[1], 64, stride=9), :] = block[64 * i : 64 * i + 64]
    out2[...] = deep_sum[...]


def on_device(images, first_weight, deep_weight, deep_cotangent):
    anywhere = pl.BlockSpec(memory_space=pltpu.HBM)
    vmem = pl.BlockSpec(memory_space=pltpu.VMEM)

    def dma(count):
        return [pltpu.SemaphoreType.DMA((count,))] * 2

    first, deep = pl.pallas_call(
        kernel,
        out_shape=(jax.ShapeDtypeStruct((128, 640), BF), jax.ShapeDtypeStruct((32, 144), F32)),
        in_specs=[anywhere] * 4,
        out_specs=(vmem, vmem),
        scratch_shapes=[
            pltpu.VMEM((80, 4352), BF),
            pltpu.VMEM((576, 128), BF),
            pltpu.VMEM((32, 1152), BF),
            pltpu.VMEM((32, 16, 128), BF),
            pltpu.VMEM((7, 17, 16, 256), BF),
            pltpu.VMEM((576, 128), F32),
            pltpu.VMEM((3, 256, 128), BF),
            pltpu.VMEM((1152, 128), F32),
            pltpu.VMEM((256, 1152), BF),
            pltpu.VMEM((512, 128), F32),
            pltpu.VMEM((4, 128, 128), BF),
            pltpu.VMEM((8, 4, 16, 128), BF),
            pltpu.VMEM((2, 256, 128), F32),
            pltpu.VMEM((3, 17, 16, 128), BF),
            pltpu.VMEM((3, 16, 16, 128), BF),
            pltpu.VMEM((3, 17, 16, 128), F32),
            pltpu.VMEM((3, 16, 16, 128), F32),
            pltpu.VMEM((256, 1152), BF),
            pltpu.VMEM((9, 4, 2, 16, 256), BF),
            pltpu.VMEM((9, 4, 16, 256), BF),
            pltpu.VMEM((9, 4, 16, 256), BF),
            pltpu.VMEM((4, 9, 16, 256), BF),
            pltpu.VMEM((128, 640), BF),
            pltpu.VMEM((8, 16, 640), BF),
            pltpu.VMEM((8, 3, 16, 128), BF),
            pltpu.VMEM((16, 3, 16, 128), BF),
            pltpu.VMEM((16, 640), BF),
            pltpu.VMEM((16, 16, 640), BF),
            pltpu.VMEM((128, 640), BF),
            pltpu.VMEM((256, 128), F32),
            pltpu.SemaphoreType.DMA((4,)),
            *dma(3), *dma(7), *dma(7), *dma(7), *dma(1), *dma(4), *dma(16), *dma(8), *dma(16), *dma(8),
        ],
        compiler_params=pltpu.CompilerParams(
            collective_id=0, has_side_effects=True, vmem_limit_bytes=40 * 2**20
        ),
    )(*(pltpu.with_memory_space_constraint(v, pltpu.HBM) for v in (images, first_weight, deep_weight.T, deep_cotangent)))
    first, deep = pl.pallas_call(
        finish,
        out_shape=(jax.ShapeDtypeStruct((576, 128), F32), jax.ShapeDtypeStruct((32, 144), F32)),
        in_specs=[vmem, vmem],
        out_specs=(vmem, vmem),
        compiler_params=pltpu.CompilerParams(vmem_limit_bytes=40 * 2**20),
    )(first, deep)
    return first, deep.T


def solution(mesh):
    return jax.shard_map(
        on_device,
        mesh=mesh,
        in_specs=(P("sample", "row", "col"), P(), P(None, "col"), P("sample", "col", "row", None)),
        out_specs=(P(), P("row", "col")),
        check_vma=False,
    )
```

```python
import jax
import jax.numpy as jnp
from jax import lax
from jax.experimental import pallas as pl
from jax.experimental.pallas import tpu as pltpu
from jax.sharding import PartitionSpec as P

BF = jnp.bfloat16
F32 = jnp.float32
MESH = pl.DeviceIdType.MESH

HOPS = {(0, 0): 0, (0, 1): 1, (1, 1): 1, (1, 0): 2}
PLANE = sorted(
    ((dz, fx, fs) for dz in range(4) for fx in range(2) for fs in range(2) if dz + fx + fs),
    key=lambda step: -(min(step[0], 4 - step[0]) + HOPS[step[1:]]),
)
LINE = (4, 5, 3, 2, 6, 7, 1)
N_ROW = 8
N_COL = 8
N_BOTH = 16


def nn(a, b):
    return lax.dot_general(a, b, (((1,), (0,)), ((), ())), preferred_element_type=F32)


def nt(a, b):
    return lax.dot_general(a, b, (((1,), (1,)), ((), ())), preferred_element_type=F32)


def tn(a, b):
    return lax.dot_general(a, b, (((0,), (0,)), ((), ())), preferred_element_type=F32)


def eye(size):
    i = lax.broadcasted_iota(jnp.int32, (size, size), 0)
    j = lax.broadcasted_iota(jnp.int32, (size, size), 1)
    return (i == j).astype(F32).astype(BF)


def rows_of(index, size):
    return pl.ds(pl.multiple_of(index * size, size), size)


def remote(src, dst, send, recv, device):
    return pltpu.make_async_remote_copy(
        src_ref=src, dst_ref=dst, send_sem=send, recv_sem=recv, device_id=device, device_id_type=MESH
    )


class Fan:
    def __init__(self, pairs):
        self.pairs = list(pairs)

    def start(self):
        for out, _ in self.pairs:
            out.start()

    def wait_recv(self):
        for _, arriving in self.pairs:
            arriving.wait_recv()

    def wait_send(self):
        for out, _ in self.pairs:
            out.wait_send()


def kernel(
    img, w1, wd, cot, first_sum, deep_sum,
    xe, w1v, wdv, cotv, xr, w1f, wf, wdf, wt, cotf, cs, cr, q, acte, acto, sle, slo, patch,
    gw, pair_in, half, ra, gt, fa, sb, rb, sb2, rb2, o2,
    in_sem, halo_s, halo_r, w_s, w_r, v_s, v_r, c_s, c_r, d0_s, d0_r, d1_s, d1_r, d2_s, d2_r,
    f1_s, f1_r, f2_s, f2_r, f3_s, f3_r,
):
    s, r, c = (lax.axis_index(name) for name in ("sample", "row", "col"))
    core = lax.rem(r, 2)
    partner = r + 1 - 2 * core
    plane = s * N_COL + c

    inputs = [
        pltpu.make_async_copy(cot.at[0], cotv, in_sem.at[0]),
        pltpu.make_async_copy(wd, wdv, in_sem.at[1]),
        pltpu.make_async_copy(w1, w1v, in_sem.at[2]),
        pltpu.make_async_copy(img.at[0], xe.at[pl.ds(16, 64), pl.ds(256, 4096)], in_sem.at[3]),
    ]

    z, xhi = c // 2, lax.rem(c, 2)

    def in_plane(step, sign=1):
        dz, fx, fs = step
        return lax.rem(s + fs, 2), lax.rem(z + 4 + sign * dz, 4) * 2 + lax.rem(xhi + fx, 2)

    down, right = lax.rem(r + 1, N_ROW), lax.rem(c + 1, N_COL)

    barrier = pltpu.get_barrier_semaphore()
    greeted = []
    for step in PLANE:
        ps, pc = in_plane(step)
        greeted.append((ps, r, pc))
    for k in LINE:
        greeted.append((s, lax.rem(r + k, N_ROW), c))
    for device in greeted:
        pl.semaphore_signal(barrier, inc=1, device_id=device, device_id_type=MESH)
    for copy in inputs:
        copy.start()

    unit = eye(128)

    inputs[0].wait()
    cotf[...] = cotv[...].reshape(512, 128).astype(F32)
    for g in range(4):
        picked = [cotf[pl.ds(4 * g + k, 32, stride=16), :] for k in range(4)]
        cs[g] = nt(unit, jnp.concatenate(picked, 0).astype(BF)).astype(BF)
    cr[0] = cs[:, rows_of(c, 16), :]

    inputs[1].wait()
    blank = jnp.zeros((96, 128), BF)
    for j in range(9):
        wdf[128 * j : 128 * j + 128] = nt(unit, jnp.concatenate([wdv[:, 128 * j : 128 * j + 128], blank], 0))
    for tap in range(9):
        piece = wdf[pl.ds(tap, 128, stride=9), :].astype(BF)
        wt[rows_of(c, 32), 128 * tap : 128 * tap + 128] = nt(unit, piece)[0:32].astype(BF)

    inputs[2].wait()
    w1f[...] = w1v[...].astype(F32)
    for ta in range(3):
        wf[ta, 0:64] = jnp.zeros((64, 128), BF)
        for tb in range(3):
            wf[ta, 64 * tb + 64 : 64 * tb + 128] = w1f[pl.ds(3 * ta + tb, 64, stride=9), :].astype(BF)

    pl.semaphore_wait(barrier, len(greeted))

    def halo(index, source, target, device):
        return remote(source, target, halo_s.at[index], halo_r.at[index], device)

    to_down = halo(0, img.at[0, pl.ds(48, 16), :], xe.at[pl.ds(0, 16), pl.ds(256, 4096)], (s, down, c))
    to_right = halo(1, img.at[0, :, pl.ds(3840, 256)], xe.at[pl.ds(16, 64), pl.ds(0, 256)], (s, r, right))
    to_corner = halo(2, xe.at[pl.ds(64, 16), pl.ds(0, 256)], xe.at[pl.ds(0, 16), pl.ds(0, 256)], (s, down, c))
    sends_down, sends_right = r < N_ROW - 1, c < N_COL - 1
    has_up, has_left = r > 0, c > 0

    def across(dz, dx, sign=1):
        return in_plane((dz, dx, dx), sign)

    def half_shard(col, which):
        return wt.at[pl.ds(pl.multiple_of(32 * col + 16 * which, 16), 16), :]

    far_first = ((2, 1), (1, 1), (3, 1), (2, 0), (1, 0), (3, 0), (0, 1))
    weights, handed_on = [], []
    for k, (dz, dx) in enumerate(far_first):
        ps, pc = across(dz, dx)
        qs, qc = across(dz, dx, -1)
        weights.append(
            (
                remote(half_shard(c, core), half_shard(c, core), w_s.at[k], w_r.at[k], (ps, r, pc)),
                remote(half_shard(qc, core), half_shard(qc, core), w_s.at[k], w_r.at[k], (qs, r, qc)),
            )
        )
        handed_on.append(
            (
                remote(half_shard(qc, core), half_shard(qc, core), v_s.at[k], v_r.at[k], (s, partner, c)),
                remote(half_shard(qc, 1 - core), half_shard(qc, 1 - core), v_s.at[k], v_r.at[k], (s, partner, c)),
            )
        )
    weights, handed_on = Fan(weights), Fan(handed_on)
    weights.start()

    @pl.when(sends_right)
    def _():
        to_right.start()

    @pl.when(sends_down)
    def _():
        to_down.start()

    cotangents = []
    for k, (dz, dx) in enumerate(far_first):
        _, pc = across(dz, dx)
        _, qc = across(dz, dx, -1)
        cotangents.append(
            (
                remote(cs.at[:, rows_of(pc, 16), :], cr.at[dz + 4 * dx], c_s.at[k], c_r.at[k], (s, r, pc)),
                remote(cs.at[:, rows_of(qc, 16), :], cr.at[dz + 4 * dx], c_s.at[k], c_r.at[k], (s, r, qc)),
            )
        )
    cotangents = Fan(cotangents)

    @pl.when(jnp.logical_not(has_up))
    def _():
        xe[0:16, 256:4352] = jnp.zeros((16, 4096), BF)

    @pl.when(jnp.logical_not(has_left))
    def _():
        xe[16:80, 0:256] = jnp.zeros((64, 256), BF)

    @pl.when(jnp.logical_not(jnp.logical_and(has_up, has_left)))
    def _():
        xe[0:16, 0:256] = jnp.zeros((16, 256), BF)

    inputs[3].wait()

    @pl.when(has_up)
    def _():
        to_down.wait_recv()

    cotangents.start()
    row = lax.broadcasted_iota(jnp.int32, (112, 80), 0)
    col = lax.broadcasted_iota(jnp.int32, (112, 80), 1)
    pick = (col == 13 + 4 * (row % 16) + row // 16).astype(F32).astype(BF)

    def select(t):
        xr[:, t] = nn(pick, xe[:, 256 * t : 256 * t + 256]).astype(BF).reshape(7, 16, 256)

    for t in range(1, 17):
        select(t)

    @pl.when(has_left)
    def _():
        to_right.wait_recv()

    @pl.when(jnp.logical_and(sends_down, has_left))
    def _():
        to_corner.start()

    for k in range(6, -1, -1):
        weights.pairs[k][1].wait_recv()
        handed_on.pairs[k][0].start()

    @pl.when(jnp.logical_and(has_up, has_left))
    def _():
        to_corner.wait_recv()

    select(0)

    def even_of(p):
        return xr[p].reshape(272, 256)

    def odd_of(p):
        return jnp.concatenate([xr[p, 0:16, :, 128:256], xr[p, 1:17, :, 0:128]], 2).reshape(256, 256)

    for a in range(3):
        even = nn(even_of(2 * a), wf[0]) + nn(even_of(2 * a + 1), wf[1]) + nn(even_of(2 * a + 2), wf[2])
        odd = nn(odd_of(2 * a), wf[0]) + nn(odd_of(2 * a + 1), wf[1]) + nn(odd_of(2 * a + 2), wf[2])
        for pre, act, slope, count in ((even, acte, sle, 17), (odd, acto, slo, 16)):
            sig = jax.nn.sigmoid(pre)
            act[a] = (pre * sig).astype(BF).reshape(count, 16, 128)
            slope[a] = (sig * (1.0 + pre * (1.0 - sig))).reshape(count, 16, 128)

    for a in range(3):
        patch[:, 384 * a : 384 * a + 128] = acte[a, 0:16].reshape(256, 128)
        patch[:, 384 * a + 128 : 384 * a + 256] = acto[a].reshape(256, 128)
        patch[:, 384 * a + 256 : 384 * a + 384] = acte[a, 1:17].reshape(256, 128)

    cotangents.wait_recv()
    quarter = lax.broadcasted_iota(jnp.int32, (16, 128), 1) // 32
    def from_col(col):
        return lax.rem(z + 4 - col // 2, 4) + 4 * lax.rem(xhi + col % 2, 2)

    for half_of in range(2):
        slots = [from_col(4 * half_of + i) for i in range(4)]
        for g in range(4):
            tiles = [cr[slots[i], g].astype(F32) for i in range(4)]
            for k in range(4):
                mixed = jnp.zeros((16, 128), F32)
                for i in range(4):
                    shift = (32 * (i - k)) % 128
                    moved = pltpu.roll(tiles[i], shift, 1) if shift else tiles[i]
                    mixed = jnp.where(quarter == i, moved, mixed)
                q[half_of, 16 * (4 * g + k) : 16 * (4 * g + k) + 16] = mixed
    cotangent = jnp.concatenate(
        [jnp.concatenate([q[h, pl.ds(n, 16, stride=16), :] for h in range(2)], 1) for n in range(16)], 0
    )

    handed_on.wait_recv()
    pre = nt(patch[...], wt[...])
    sig = jax.nn.sigmoid(pre)
    dg = (cotangent * (sig * (1.0 + pre * (1.0 - sig)))).astype(BF)

    back = nn(dg, wt[...])
    empty = jnp.zeros((1, 16, 128), F32)
    totals = [jnp.zeros((128, 256), F32) for _ in range(3)]
    edge = []
    for a in range(3):
        part = [back[:, 384 * a + 128 * b : 384 * a + 128 * b + 128].reshape(16, 16, 128) for b in range(3)]
        even = jnp.concatenate([part[0], empty], 0) + jnp.concatenate([empty, part[2]], 0)
        odd = part[1]
        if a == 1:
            even, odd = even.astype(BF).astype(F32), odd.astype(BF).astype(F32)
        even = (even * sle[a]).reshape(272, 128).astype(BF)
        odd = (odd * slo[a]).reshape(256, 128).astype(BF)
        edge.append(even[0:16])
        for ta in range(3):
            inner = xr[2 * a + ta, 1:17].reshape(256, 256)
            totals[ta] += tn(even[16:272], inner) + tn(odd, odd_of(2 * a + ta))
    edge = jnp.concatenate(edge, 0)
    for ta in range(3):
        totals[ta] += tn(edge, jnp.concatenate([xr[2 * a + ta, 0] for a in range(3)], 0))
    for ta in range(3):
        gt[:, 128 * ta : 128 * ta + 128] = totals[ta][:, 128:256].astype(BF)
    low = lax.broadcasted_iota(jnp.int32, (128, 128), 1) < 64
    both = jnp.where(low, pltpu.roll(totals[1][:, 0:128], 64, 1), totals[0][:, 0:128])
    gt[:, 384:512] = both.astype(BF)
    gt[:, 512:640] = totals[2][:, 0:128].astype(BF)

    first1 = []
    for k in LINE:
        pr, qr = lax.rem(r + k, N_ROW), lax.rem(r + N_ROW - k, N_ROW)
        first1.append(
            (
                remote(gt.at[rows_of(pr, 16), :], fa.at[k], f1_s.at[k], f1_r.at[k], (s, pr, c)),
                remote(gt.at[rows_of(qr, 16), :], fa.at[k], f1_s.at[k], f1_r.at[k], (s, qr, c)),
            )
        )
    first1 = Fan(first1)
    first1.start()

    gw[...] = tn(patch[...], dg).astype(BF).reshape(9, 4, 2, 16, 256)
    pair = remote(gw.at[:, :, 1 - core], pair_in, d0_s.at[0], d0_r.at[0], (s, partner, c))
    pair.start()
    pair.wait_recv()
    half[...] = (gw[:, :, core].astype(F32) + pair_in[...].astype(F32)).astype(BF)

    y = r // 2
    deep1 = []
    for k in (2, 1, 3):
        py, qy = lax.rem(y + k, 4), lax.rem(y + 4 - k, 4)
        deep1.append(
            (
                remote(half.at[:, py], ra.at[k], d1_s.at[k], d1_r.at[k], (s, 2 * py + core, c)),
                remote(half.at[:, qy], ra.at[k], d1_s.at[k], d1_r.at[k], (s, 2 * qy + core, c)),
            )
        )
    deep1 = Fan(deep1)

    first1.wait_recv()
    total = gt[rows_of(r, 16), :].astype(F32)
    for k in range(1, N_ROW):
        total = total + fa[k].astype(F32)
    sb2[...] = total.astype(BF)
    first2 = []
    for k, step in enumerate(PLANE):
        ps, pc = in_plane(step)
        qs, qc = in_plane(step, -1)
        first2.append(
            (
                remote(sb2, rb2.at[plane], f2_s.at[k], f2_r.at[k], (ps, r, pc)),
                remote(sb2, rb2.at[qs * N_COL + qc], f2_s.at[k], f2_r.at[k], (qs, r, qc)),
            )
        )
    first2 = Fan(first2)
    first2.start()
    deep1.start()
    rb2[plane] = sb2[...]

    deep1.wait_recv()
    total = half[:, y].astype(F32)
    for k in range(1, 4):
        total = total + ra[k].astype(F32)
    for h in range(2):
        block = total[0:8, :, 128 * h : 128 * h + 128].reshape(128, 128)
        sb[4 * h : 4 * h + 4, 0:2] = nt(unit, block.astype(BF)).astype(BF).reshape(4, 2, 16, 128)
        last = total[8, :, 128 * h : 128 * h + 128]
        for p in range(4):
            moved = pltpu.roll(last, 128 - 32 * p, 1) if p else last
            sb[4 * h + p, 2] = moved.astype(BF)
    deep2 = []
    for k, step in enumerate(PLANE):
        ps, pc = in_plane(step)
        qs, qc = in_plane(step, -1)
        deep2.append(
            (
                remote(sb.at[pc], rb.at[plane], d2_s.at[k], d2_r.at[k], (ps, r, pc)),
                remote(sb.at[qc], rb.at[qs * N_COL + qc], d2_s.at[k], d2_r.at[k], (qs, r, qc)),
            )
        )
    deep2 = Fan(deep2)
    deep2.start()
    rb[plane] = sb[c]

    @pl.when(sends_down)
    def _():
        to_down.wait_send()

    @pl.when(sends_right)
    def _():
        to_right.wait_send()

    @pl.when(jnp.logical_and(sends_down, has_left))
    def _():
        to_corner.wait_send()

    pair.wait_send()
    for fan in (weights, handed_on, cotangents, first1, deep1):
        fan.wait_send()

    first2.wait_recv()
    total = rb2[0].astype(F32)
    for p in range(1, N_BOTH):
        total = total + rb2[p].astype(F32)
    first_sum[rows_of(r, 16), :] = total.astype(BF)
    first3 = []
    for k in LINE:
        pr, qr = lax.rem(r + k, N_ROW), lax.rem(r + N_ROW - k, N_ROW)
        first3.append(
            (
                remote(first_sum.at[rows_of(r, 16), :], first_sum.at[rows_of(r, 16), :], f3_s.at[k], f3_r.at[k], (s, pr, c)),
                remote(first_sum.at[rows_of(qr, 16), :], first_sum.at[rows_of(qr, 16), :], f3_s.at[k], f3_r.at[k], (s, qr, c)),
            )
        )
    first3 = Fan(first3)
    first3.start()

    deep2.wait_recv()
    total = rb[0].astype(F32)
    for p in range(1, N_BOTH):
        total = total + rb[p].astype(F32)
    most = jnp.concatenate([total[0], total[1], jnp.zeros((96, 128), F32)], 0).T
    for tap in range(9):
        o2[pl.ds(tap, 16, stride=9), :] = most[16 * tap : 16 * tap + 16] if tap < 8 else total[2]
    deep_sum[...] = o2[...].T[0:32, 0:144]

    for fan in (first2, deep2):
        fan.wait_send()
    first3.wait_recv()

    first3.wait_send()


def finish(first_sum, deep_sum, out1, out2):
    unit = eye(128)
    places = ((0, 1), (0, 2), (1, 1), (1, 2), (2, 1), (2, 2), (1, 0), (0, 0), None, (2, 0))
    for j in range(5):
        block = nt(unit, first_sum[:, 128 * j : 128 * j + 128])
        for i in range(2):
            place = places[2 * j + i]
            if place is not None:
                out1[pl.ds(3 * place[0] + place[1], 64, stride=9), :] = block[64 * i : 64 * i + 64]
    out2[...] = deep_sum[...]


def on_device(images, first_weight, deep_weight, deep_cotangent):
    anywhere = pl.BlockSpec(memory_space=pltpu.HBM)
    vmem = pl.BlockSpec(memory_space=pltpu.VMEM)

    def dma(count):
        return [pltpu.SemaphoreType.DMA((count,))] * 2

    first, deep = pl.pallas_call(
        kernel,
        out_shape=(jax.ShapeDtypeStruct((128, 640), BF), jax.ShapeDtypeStruct((32, 144), F32)),
        in_specs=[anywhere] * 4,
        out_specs=(vmem, vmem),
        scratch_shapes=[
            pltpu.VMEM((80, 4352), BF),
            pltpu.VMEM((576, 128), BF),
            pltpu.VMEM((32, 1152), BF),
            pltpu.VMEM((32, 16, 128), BF),
            pltpu.VMEM((7, 17, 16, 256), BF),
            pltpu.VMEM((576, 128), F32),
            pltpu.VMEM((3, 256, 128), BF),
            pltpu.VMEM((1152, 128), F32),
            pltpu.VMEM((256, 1152), BF),
            pltpu.VMEM((512, 128), F32),
            pltpu.VMEM((4, 128, 128), BF),
            pltpu.VMEM((8, 4, 16, 128), BF),
            pltpu.VMEM((2, 256, 128), F32),
            pltpu.VMEM((3, 17, 16, 128), BF),
            pltpu.VMEM((3, 16, 16, 128), BF),
            pltpu.VMEM((3, 17, 16, 128), F32),
            pltpu.VMEM((3, 16, 16, 128), F32),
            pltpu.VMEM((256, 1152), BF),
            pltpu.VMEM((9, 4, 2, 16, 256), BF),
            pltpu.VMEM((9, 4, 16, 256), BF),
            pltpu.VMEM((9, 4, 16, 256), BF),
            pltpu.VMEM((4, 9, 16, 256), BF),
            pltpu.VMEM((128, 640), BF),
            pltpu.VMEM((8, 16, 640), BF),
            pltpu.VMEM((8, 3, 16, 128), BF),
            pltpu.VMEM((16, 3, 16, 128), BF),
            pltpu.VMEM((16, 640), BF),
            pltpu.VMEM((16, 16, 640), BF),
            pltpu.VMEM((256, 128), F32),
            pltpu.SemaphoreType.DMA((4,)),
            *dma(3), *dma(7), *dma(7), *dma(7), *dma(1), *dma(4), *dma(16), *dma(8), *dma(16), *dma(8),
        ],
        compiler_params=pltpu.CompilerParams(
            collective_id=0, has_side_effects=True, vmem_limit_bytes=40 * 2**20
        ),
    )(*(pltpu.with_memory_space_constraint(v, pltpu.HBM) for v in (images, first_weight, deep_weight.T, deep_cotangent)))
    first, deep = pl.pallas_call(
        finish,
        out_shape=(jax.ShapeDtypeStruct((576, 128), F32), jax.ShapeDtypeStruct((32, 144), F32)),
        in_specs=[vmem, vmem],
        out_specs=(vmem, vmem),
        compiler_params=pltpu.CompilerParams(vmem_limit_bytes=40 * 2**20),
    )(first, deep)
    return first, deep.T


def solution(mesh):
    return jax.shard_map(
        on_device,
        mesh=mesh,
        in_specs=(P("sample", "row", "col"), P(), P(None, "col"), P("sample", "col", "row", None)),
        out_specs=(P(), P("row", "col")),
        check_vma=False,
    )
```
